32 devices in a mesh: gx: 4 (over y, x), gy: 2 (over core), gz: 4 (over z).
Axes of the slice: x: 2, y: 2, z: 4, core: 2. Of those that a mesh axis runs over, the one named last changes fastest.
Arguments:
- basis: bfloat16 [8, 3, 16, 512, 128], P('gx', None, 'gy', 'gz'), may hold values from -4.8 to 4.8
- modal_now: bfloat16 [128, 8], replicated, may hold values from -0.5 to 0.5
- modal_prev: bfloat16 [128, 8], replicated, may hold values from -0.5 to 0.5
- material_ids: int32 [8, 16, 512], P('gx', 'gy', 'gz'), may hold values from 0 to 3
- moduli: float32 [3, 4], replicated, may hold values from 0.4 to 1.6
- drive_mask: int32 [8, 8, 16, 512], P(None, 'gx', 'gy', 'gz'), may hold values 0 or 1
- drive: float32 [3, 8], replicated, may hold values from -8 to 8
Outputs:
- displacement: float32 [3, 8, 8, 16, 512], P(None, None, 'gx', 'gy', 'gz')
- modes: float32 [3, 8, 8, 16, 512], P(None, None, 'gx', 'gy', 'gz')
- coefficients: float32 [4, 2, 128, 8], replicated
- rfactor: float32 [4, 8, 8], replicated
The draws below stay inside these ranges and needn't reach their ends.
All inputs are finite; a program needn't handle non-finite values. No bound on the sum of `drive_mask` on one device may be relied on, other than what follows from the above.
Results may differ from the reference program's by a relative error of at most 0.0008.
The reference program's roundings to bfloat16 on the way (of `snapshot`) count: a program that leaves them out, or rounds other values in their place, can miss the bound.
Values sent between devices are 32-bit elements; how exact they have to be, the bound alone decides.
A program may use at most 128 MiB of HBM per device.

```python
import math
import jax
import jax.numpy as jnp
from jax import lax

MODES = 128
CASES = 8
NMAT = 4
STEPS = 4
NX = 8
NY = 16
NZ = 512


def draw_basis(key, part):
    first_key, second_key = jax.random.split(jax.random.fold_in(key, 11))
    shape = (NX, 3, NY, NZ, MODES)
    scales = 0.8 + 0.4 * jax.random.uniform(second_key, (MODES,), jnp.float32)
    values = jax.random.truncated_normal(first_key, -4.0, 4.0, shape, jnp.float32)
    return (values * scales).astype(jnp.bfloat16)


def place_ends(values, stream_key, least, high):
    spot = [jax.random.randint(jax.random.fold_in(stream_key, axis), (), 0, length) for axis, length in enumerate(values.shape)]
    longest = values.shape.index(max(values.shape))
    next_to = spot[:longest] + [(spot[longest] + 1) % values.shape[longest]] + spot[longest + 1:]
    return values.at[tuple(spot)].set(least).at[tuple(next_to)].set(high)


def bell_draw(rng, dims, spread, limit, held_as=jnp.bfloat16):
    values = jax.random.normal(rng, dims, jnp.float32) * spread
    return jnp.minimum(jnp.maximum(values, -limit), limit).astype(held_as)


def setup_inputs(seed: int = 0) -> dict:
    key_of = jax.random.split(jax.random.key(seed), 8)
    return {
        "basis": draw_basis(jax.random.fold_in(key_of[7], 71), 0),
        "modal_now": bell_draw(key_of[1], (MODES, CASES), MODES ** -0.5, 0.5),
        "modal_prev": bell_draw(key_of[2], (MODES, CASES), MODES ** -0.5, 0.5),
        "material_ids": place_ends(jax.random.randint(key_of[3], (NX, NY, NZ), 0, NMAT), jax.random.fold_in(key_of[3], 1), 0, NMAT - 1).astype(jnp.int32),
        "moduli": jnp.clip(jnp.exp(jax.random.uniform(key_of[4], (3, NMAT), jnp.float32, math.log(0.4), math.log(1.6))), 0.4, 1.6),
        "drive_mask": place_ends((jax.random.randint(key_of[5], (CASES, NX, NY, NZ), 0, 8) < 1).astype(jnp.int32), jax.random.fold_in(key_of[5], 1), 0, 1),
        "drive": bell_draw(key_of[6], (3, CASES), 2.0, 8.0, jnp.float32),
    }


step_squared = 0.1
ramp_steps = 4.0

def interior(array, direction_axis, offset):
    base_axis = array.ndim - 3
    result = array
    for axis_index in range(3):
        extent = array.shape[base_axis + axis_index]
        begin = offset if axis_index == direction_axis else 1
        result = lax.slice_in_dim(result, begin, extent - 2 + begin, axis=base_axis + axis_index)
    return result

def stiffness(field, material_props):
    component_rows = []
    for component in range(3):
        center = interior(field[component], 0, 1)
        accumulated = jnp.zeros_like(center)
        for direction_axis in range(3):
            modulus = material_props[0] if component == direction_axis else material_props[1]
            center_modulus = interior(modulus, 0, 1)
            for offset in (0, 2):
                coupling = 0.5 * (center_modulus + interior(modulus, direction_axis, offset))
                accumulated = accumulated + coupling * (center - interior(field[component], direction_axis, offset))
        component_rows.append(accumulated)
    return jnp.stack(component_rows)

def lookup(material_ids, moduli):
    levels = jnp.arange(moduli.shape[1], dtype=jnp.int32)
    onehot = (material_ids[None] == levels[:, None, None, None]).astype(moduli.dtype)
    return jnp.einsum('mxyz,pm->pxyz', onehot, moduli, precision=lax.Precision.HIGHEST)

def expand(basis, coefficient):
    weights = coefficient.astype(jnp.float32)

    def per_slab(basis_slab):
        return jnp.einsum('cyzk,kj->cjyz', basis_slab.astype(jnp.float32), weights, precision=lax.Precision.HIGHEST)
    slabs = lax.map(per_slab, basis)
    return jnp.moveaxis(slabs, 0, 2)

def project(basis, field):
    moved = jnp.moveaxis(field, 2, 0)

    def per_slab(running, pair_slabs):
        basis_slab, field_slab = pair_slabs
        return (running + jnp.einsum('cyzk,cjyz->kj', basis_slab.astype(jnp.float32), field_slab.astype(jnp.float32), precision=lax.Precision.HIGHEST), None)
    start = jnp.zeros((basis.shape[4], field.shape[1]), jnp.float32)
    running, unused = lax.scan(per_slab, start, (basis, moved))
    return running

def gram_of(block, dof_weight):
    return jnp.einsum('cixyz,cjxyz->ij', block, block, precision=lax.Precision.HIGHEST) * dof_weight

def apply_inverse(block, lower_factor):
    identity_block = jnp.eye(lower_factor.shape[0], dtype=lower_factor.dtype)
    lower_inverse = jax.scipy.linalg.solve_triangular(lower_factor, identity_block, lower=True)
    return jnp.einsum('cixyz,ji->cjxyz', block, lower_inverse, precision=lax.Precision.HIGHEST)

def reference(basis, modal_now, modal_prev, material_ids, moduli, drive_mask, drive):
    dof_weight = 1.0 / (3.0 * NX * NY * NZ)
    current = expand(basis, modal_now)
    earlier = expand(basis, modal_prev)
    material_props = lookup(material_ids, moduli)
    props_padded = jnp.pad(material_props, ((0, 0), (1, 1), (1, 1), (1, 1)))
    port_mask = drive_mask.astype(jnp.float32)
    coefficient_list = []
    factor_list = []
    modes = current
    for step in range(STEPS):
        ramp_level = min(1.0, (step + 1) / ramp_steps)
        padded = jnp.pad(current, ((0, 0), (0, 0), (1, 1), (1, 1), (1, 1)))
        load_field = drive[:, :, None, None, None] * port_mask[None] * ramp_level
        following = 2.0 * current - earlier + step_squared * material_props[2] * (load_field - stiffness(padded, props_padded))
        earlier = current
        current = following
        snapshot = following.astype(jnp.bfloat16)
        first_coef = project(basis, snapshot) * dof_weight
        first_resid = snapshot.astype(jnp.float32) - expand(basis, first_coef.astype(jnp.bfloat16))
        first_lower = jnp.linalg.cholesky(gram_of(first_resid, dof_weight))
        first_q = apply_inverse(first_resid, first_lower)
        second_coef = project(basis, first_q.astype(jnp.bfloat16)) * dof_weight
        second_resid = first_q - expand(basis, second_coef.astype(jnp.bfloat16))
        second_lower = jnp.linalg.cholesky(gram_of(second_resid, dof_weight))
        modes = apply_inverse(second_resid, second_lower)
        coefficient_list.append(jnp.stack([first_coef, second_coef]))
        factor_list.append(jnp.dot(first_lower, second_lower, precision=lax.Precision.HIGHEST).T)
    return (current, modes, jnp.stack(coefficient_list), jnp.stack(factor_list))
```

```python
import functools
import jax
import jax.numpy as jnp
from jax import lax
from jax.experimental import pallas as pl
from jax.experimental.pallas import tpu as pltpu
from jax.sharding import PartitionSpec as P

STEPS = 4
MESH_IDS = pl.DeviceIdType.MESH
AXES = ("gx", "gy", "gz")
HIGHEST = lax.Precision.HIGHEST
NT = (((1,), (1,)), ((), ()))
NN = (((1,), (0,)), ((), ()))
TN = (((0,), (0,)), ((), ()))

step_squared = 0.1
ramp_steps = 4.0


def dot32(a, b, dims):
    return lax.dot_general(a, b, dims, precision=HIGHEST, preferred_element_type=jnp.float32)


def dot16(a, b, dims):
    return lax.dot_general(a, b, dims, preferred_element_type=jnp.float32)


def small_product(a, b):
    total = a[:, :, 0:1] * b[:, 0:1, :]
    for k in range(1, b.shape[1]):
        total = total + a[:, :, k : k + 1] * b[:, k : k + 1, :]
    return total


def factor(gram):
    s, n, _ = gram.shape
    rows = lax.broadcasted_iota(jnp.int32, (s, n, 128), 1)
    lanes = lax.broadcasted_iota(jnp.int32, (s, n, 128), 2)
    work = jnp.concatenate([gram, jnp.zeros((s, n, 128 - n), jnp.float32)], axis=2)
    work = jnp.where(lanes == rows + n, 1.0, work)
    pivots = jnp.ones((s, n, 128), jnp.float32)
    for k in range(n):
        pivot = work[:, k : k + 1, k : k + 1]
        pivots = jnp.where(rows == k, pivot, pivots)
        if k < n - 1:
            ratio = jnp.where(rows > k, work[:, :, k : k + 1] / pivot, 0.0)
            work = work - ratio * work[:, k : k + 1, :]
    work = work * lax.rsqrt(pivots)
    upper = jnp.where(lanes >= rows, work, 0.0)[:, :, :n]
    return upper, work[:, :, n : 2 * n]


def kernel(sizes, basis_ref, now_ref, prev_ref, ids_ref, moduli_ref, mask_ref, drive_ref,
           disp_ref, modes_ref, coef_ref, rfac_ref,
           field_ref, ids_field_ref, hx_ref, hy_ref, hz_ref, zs_ref,
           ix_ref, iy_ref, iz_ref, izs_ref, coup_ref,
           gpart_ref, gy_buf, gx_buf, gz_buf, gslice_ref, gfull_ref,
           s0y, s0x, s0z, s1y, s1x, s1z, stat_ref,
           halo_send, halo_recv, g_send, g_recv, s_send, s_recv):
    nx, ny, nz = sizes
    count = dict(zip(AXES, sizes))
    me = {axis: lax.axis_index(axis) for axis in AXES}
    X, C, Y, Z, K = basis_ref.shape
    J = now_ref.shape[1]
    tiles = X * C * Y
    weight = 1.0 / (tiles * Z * nx * ny * nz)

    hx_ref[...] = jnp.zeros_like(hx_ref)
    hy_ref[...] = jnp.zeros_like(hy_ref)
    hz_ref[...] = jnp.zeros_like(hz_ref)
    ix_ref[...] = jnp.zeros_like(ix_ref)
    iy_ref[...] = jnp.zeros_like(iy_ref)
    iz_ref[...] = jnp.zeros_like(iz_ref)

    barrier = pltpu.get_barrier_semaphore()
    for axis in AXES:
        for d in range(1, count[axis]):
            pl.semaphore_signal(barrier, inc=1, device_id={axis: lax.rem(me[axis] + d, count[axis])},
                                device_id_type=MESH_IDS)
    pl.semaphore_wait(barrier, nx + ny + nz - 3)

    def halo_copies(slot, src, zsrc, dst_x, dst_y, dst_z):
        plan = []
        faces = {
            "gx": (src.at[X - 1], src.at[0], dst_x),
            "gy": (src.at[:, :, Y - 1], src.at[:, :, 0], dst_y),
            "gz": (zsrc.at[1], zsrc.at[0], dst_z),
        }
        for n_axis, axis in enumerate(AXES):
            up, down, dst = faces[axis]
            for side, face in ((0, up), (1, down)):
                target = me[axis] + (1 if side == 0 else -1)
                copy = pltpu.make_async_remote_copy(
                    src_ref=face, dst_ref=dst.at[side],
                    send_sem=halo_send.at[slot, 2 * n_axis + side],
                    recv_sem=halo_recv.at[slot, 2 * n_axis + side],
                    device_id={axis: target}, device_id_type=MESH_IDS)
                has_target = (me[axis] < count[axis] - 1) if side == 0 else (me[axis] > 0)
                has_source = (me[axis] > 0) if side == 0 else (me[axis] < count[axis] - 1)
                plan.append((has_target, has_source, copy))
        return plan

    def send_all(plan):
        for has_target, _, copy in plan:
            @pl.when(has_target)
            def _(copy=copy):
                copy.start()

    def recv_all(plan):
        for _, has_source, copy in plan:
            @pl.when(has_source)
            def _(copy=copy):
                copy.wait_recv()

    def drain(plan):
        for has_target, _, copy in plan:
            @pl.when(has_target)
            def _(copy=copy):
                copy.wait_send()

    def z_faces(value, zdst):
        turned = value.reshape(-1, Z).T
        zdst[0] = turned[0:8]
        zdst[1] = turned[Z - 8 : Z]

    def neighbours(value, hx, hy, hz):
        shape = value.shape
        x_lo = jnp.concatenate([hx[0][None], value[:-1]], axis=0)
        x_hi = jnp.concatenate([value[1:], hx[1][None]], axis=0)
        y_lo = jnp.concatenate([hy[0][:, :, None], value[:, :, :-1]], axis=2)
        y_hi = jnp.concatenate([value[:, :, 1:], hy[1][:, :, None]], axis=2)
        flat = value.reshape(-1, Z)
        lanes = lax.broadcasted_iota(jnp.int32, flat.shape, 1)
        turned = jnp.concatenate(
            [hz[1], jnp.zeros((Z - 16, flat.shape[0]), jnp.float32), hz[0]], axis=0).T
        z_lo = pltpu.roll(jnp.where(lanes == Z - 1, turned, flat), 1, 1)
        z_hi = pltpu.roll(jnp.where(lanes == 0, turned, flat), Z - 1, 1)
        return ((x_lo, x_hi), (y_lo, y_hi), (z_lo.reshape(shape), z_hi.reshape(shape)))

    def exchange(axis, src_of, dst_of, send_sem, recv_sem):
        started = []
        for d in range(1, count[axis]):
            peer = lax.rem(me[axis] + d, count[axis])
            started.append(pltpu.make_async_remote_copy(
                src_ref=src_of(peer), dst_ref=dst_of(me[axis]),
                send_sem=send_sem.at[d], recv_sem=recv_sem.at[d],
                device_id={axis: peer}, device_id_type=MESH_IDS))
        for copy in started:
            copy.start()
        return started

    def finish(started):
        for copy in started:
            copy.wait_recv()
            copy.wait_send()

    def total_of(buf):
        total = buf[0]
        for i in range(1, buf.shape[0]):
            total = total + buf[i]
        return total

    idf = (ids_ref[...] + 1).astype(jnp.float32)
    idf = jnp.broadcast_to(idf[:, None, :, None, :], (X, 1, Y, J, Z))
    ids_field_ref[...] = idf
    z_faces(idf, izs_ref)
    ids_plan = halo_copies(STEPS, ids_field_ref, izs_ref, ix_ref, iy_ref, iz_ref)
    send_all(ids_plan)

    basis = basis_ref[...].reshape(tiles * Z, K)
    both = jnp.concatenate([now_ref[...], prev_ref[...]], axis=1).astype(jnp.float32)
    both = both.T.astype(jnp.bfloat16)
    start = dot16(both, basis, NT)

    def as_field(flat):
        parts = [flat[:, t * Z : (t + 1) * Z] for t in range(tiles)]
        return jnp.stack(parts).reshape(X, C, Y, J, Z)

    def as_flat(value):
        parts = value.reshape(tiles, value.shape[-2], Z)
        return jnp.concatenate([parts[t] for t in range(tiles)], axis=1)

    field_ref[1] = as_field(start[:J])
    field_ref[0] = as_field(start[J:])
    z_faces(field_ref[1], zs_ref.at[0])
    plans = [halo_copies(s, field_ref.at[s + 1], zs_ref.at[s], hx_ref.at[s], hy_ref.at[s], hz_ref.at[s])
             for s in range(STEPS)]
    send_all(plans[0])

    rows = K // ny
    gpart_ref[...] = dot16(basis, basis, TN).reshape(ny, rows, K)
    gy_buf[me["gy"]] = gpart_ref[me["gy"]]
    g_stage = exchange("gy", lambda p: gpart_ref.at[p], lambda m: gy_buf.at[m],
                       g_send.at[0], g_recv.at[0])

    recv_all(ids_plan)
    def pick(p, index):
        value = jnp.zeros_like(index)
        for m in range(moduli_ref.shape[1]):
            value = jnp.where(index == float(m + 1), moduli_ref[p, m], value)
        return value
    around = neighbours(idf, ix_ref[...], iy_ref[...], iz_ref[...])
    scale = step_squared * pick(2, idf)
    for p in range(2):
        own = pick(p, idf)
        for a in range(3):
            for side in range(2):
                coup_ref[p, a, side] = (0.5 * scale * (own + pick(p, around[a][side])))[:, 0]
    sub = lax.broadcasted_iota(jnp.int32, (J, Z), 0)
    drives = []
    for c in range(C):
        column = jnp.zeros((J, Z), jnp.float32)
        for j in range(J):
            column = jnp.where(sub == j, drive_ref[c, j], column)
        drives.append(column)
    drives = jnp.stack(drives)[None, :, None]
    mask = jnp.stack([mask_ref[:, x, y, :] for x in range(X) for y in range(Y)])
    mask = mask.astype(jnp.float32).reshape(X, 1, Y, J, Z)
    load = scale * mask * drives

    stats = {}
    bufs = ((s0y, s0x, s0z), (s1y, s1x, s1z))

    def begin_pair(pair, snap):
        proj = dot16(snap, basis, NN)
        gram = dot16(snap, snap, NT)
        gram = jnp.concatenate([gram, jnp.zeros((2 * J, K - 2 * J), jnp.float32)], axis=1)
        return jnp.concatenate([proj, gram], axis=0) * weight

    def stat_start(pair, n_axis, value):
        buf = bufs[pair][n_axis]
        axis = ("gy", "gx", "gz")[n_axis]
        stat_ref[pair, n_axis] = value
        buf[me[axis]] = value
        return exchange(axis, lambda p: stat_ref.at[pair, n_axis], lambda m: buf.at[m],
                        s_send.at[pair, n_axis], s_recv.at[pair, n_axis])

    def stat_finish(pair, n_axis, started):
        finish(started)
        return total_of(bufs[pair][n_axis])

    snaps = []
    pending = None
    for step in range(STEPS):
        recv_all(plans[step])
        current = field_ref[step + 1]
        around = neighbours(current, hx_ref[step], hy_ref[step], hz_ref[step])
        ramp = min(1.0, (step + 1) / ramp_steps)
        following = 2.0 * current - field_ref[step] + ramp * load
        for a in range(3):
            for side in range(2):
                gap = current - around[a][side]
                kind = [coup_ref[0 if c == a else 1, a, side] for c in range(C)]
                following = following - jnp.stack(kind, axis=1) * gap
        if step < STEPS - 1:
            field_ref[step + 2] = following
            z_faces(following, zs_ref.at[step + 1])
            send_all(plans[step + 1])
        snaps.append(following)
        if step == 0:
            finish(g_stage)
            gslice_ref[0] = total_of(gy_buf)
            gx_buf[me["gx"]] = gslice_ref[0]
            g_stage = exchange("gx", lambda p: gslice_ref.at[0], lambda m: gx_buf.at[m],
                               g_send.at[1], g_recv.at[1])
        if step == 1:
            snap = as_flat(jnp.concatenate(snaps, axis=3).astype(jnp.bfloat16))
            pending = stat_start(0, 0, begin_pair(0, snap))
            finish(g_stage)
            gslice_ref[1] = total_of(gx_buf)
            gz_buf[me["gz"]] = gslice_ref[1]
            g_stage = exchange("gz", lambda p: gslice_ref.at[1], lambda m: gz_buf.at[m],
                               g_send.at[2], g_recv.at[2])
            snaps = []
        if step == 2:
            pending = stat_start(0, 1, stat_finish(0, 0, pending))
            finish(g_stage)
            gslice_ref[2] = total_of(gz_buf) * weight
            gfull_ref[me["gy"]] = gslice_ref[2]
            g_stage = exchange("gy", lambda p: gslice_ref.at[2], lambda m: gfull_ref.at[m],
                               g_send.at[3], g_recv.at[3])

    snap = as_flat(jnp.concatenate(snaps, axis=3).astype(jnp.bfloat16))
    late = stat_start(1, 0, begin_pair(1, snap))
    pending = stat_start(0, 2, stat_finish(0, 1, pending))
    last = snaps[1]
    flat_last = as_flat(last)
    for x in range(X):
        for c in range(C):
            for y in range(Y):
                disp_ref[c, :, x, y, :] = last[x, c, y]
    late = stat_start(1, 1, stat_finish(1, 0, late))
    finish(g_stage)
    gram_basis = gfull_ref[...].reshape(K, K)
    first = stat_finish(0, 2, pending)
    late = stat_start(1, 2, stat_finish(1, 1, late))
    second = stat_finish(1, 2, late)

    coef1 = jnp.concatenate([first[: 2 * J], second[: 2 * J]], axis=0)
    coef1_b = coef1.astype(jnp.bfloat16).astype(jnp.float32)
    def blocks(full):
        return jnp.stack([full[J * s : J * s + J, J * s : J * s + J] for s in range(full.shape[0] // J)])
    snap_gram = jnp.concatenate(
        [blocks(first[2 * J :, : 2 * J]), blocks(second[2 * J :, : 2 * J])], axis=0)
    left = coef1 - dot32(coef1_b, gram_basis, NN)
    gram1 = snap_gram - blocks(dot32(coef1_b, left, NT) + dot32(coef1, coef1_b, NT))
    upper1, inverse1 = factor(gram1)
    coef2 = small_product(inverse1, left.reshape(STEPS, J, K)).reshape(STEPS * J, K)
    coef2_b = coef2.astype(jnp.bfloat16).astype(jnp.float32)
    left2 = coef2 - dot32(coef2_b, gram_basis, NN)
    eye = (lax.broadcasted_iota(jnp.int32, (STEPS, J, J), 1)
           == lax.broadcasted_iota(jnp.int32, (STEPS, J, J), 2)).astype(jnp.float32)
    gram2 = eye - blocks(dot32(coef2_b, left2, NT) + dot32(coef2, coef2_b, NT))
    upper2, inverse2 = factor(gram2)
    rfac_ref[...] = small_product(upper2, upper1)
    for s in range(STEPS):
        coef_ref[s, 0] = coef1[J * s : J * s + J].T
        coef_ref[s, 1] = coef2[J * s : J * s + J].T

    inv1, inv2 = inverse1[STEPS - 1 :], inverse2[STEPS - 1 :]
    tail = slice(J * (STEPS - 1), J * STEPS)
    mix = small_product(inv1, coef1_b[tail][None]) + coef2_b[tail][None]
    mix = small_product(inv2, mix)[0]
    mix_hi = mix.astype(jnp.bfloat16).astype(jnp.float32)
    parts = jnp.concatenate([mix_hi, mix - mix_hi], axis=0).astype(jnp.bfloat16)
    spread = dot16(parts, basis, NT)
    rounded = flat_last.astype(jnp.bfloat16).astype(jnp.float32)
    modes = small_product(small_product(inv2, inv1), rounded[None])[0]
    modes = modes - (spread[:J] + spread[J:])
    t = 0
    for x in range(X):
        for c in range(C):
            for y in range(Y):
                modes_ref[c, :, x, y, :] = modes[:, t * Z : (t + 1) * Z]
                t += 1

    drain(ids_plan)
    for plan in plans:
        drain(plan)


def shards(sizes, basis, modal_now, modal_prev, material_ids, moduli, drive_mask, drive):
    nx, ny, nz = sizes
    X, C, Y, Z, K = basis.shape
    J = modal_now.shape[1]
    f32 = jnp.float32
    n_flat = X * C * Y * J
    vmem = pl.BlockSpec(memory_space=pltpu.VMEM)
    smem = pl.BlockSpec(memory_space=pltpu.SMEM)
    rows = K // ny
    srows = 4 * J
    most = max(sizes)
    return pl.pallas_call(
        functools.partial(kernel, sizes),
        out_shape=(
            jax.ShapeDtypeStruct((C, J, X, Y, Z), f32),
            jax.ShapeDtypeStruct((C, J, X, Y, Z), f32),
            jax.ShapeDtypeStruct((STEPS, 2, K, J), f32),
            jax.ShapeDtypeStruct((STEPS, J, J), f32),
        ),
        in_specs=[vmem, vmem, vmem, vmem, smem, vmem, smem],
        out_specs=(vmem, vmem, vmem, vmem),
        scratch_shapes=[
            pltpu.VMEM((STEPS + 1, X, C, Y, J, Z), f32),
            pltpu.VMEM((X, 1, Y, J, Z), f32),
            pltpu.VMEM((STEPS, 2, C, Y, J, Z), f32),
            pltpu.VMEM((STEPS, 2, X, C, J, Z), f32),
            pltpu.VMEM((STEPS, 2, 8, n_flat), f32),
            pltpu.VMEM((STEPS, 2, 8, n_flat), f32),
            pltpu.VMEM((2, 1, Y, J, Z), f32),
            pltpu.VMEM((2, X, 1, J, Z), f32),
            pltpu.VMEM((2, 8, X * Y * J), f32),
            pltpu.VMEM((2, 8, X * Y * J), f32),
            pltpu.VMEM((2, 3, 2, X, Y, J, Z), f32),
            pltpu.VMEM((ny, rows, K), f32),
            pltpu.VMEM((ny, rows, K), f32),
            pltpu.VMEM((nx, rows, K), f32),
            pltpu.VMEM((nz, rows, K), f32),
            pltpu.VMEM((3, rows, K), f32),
            pltpu.VMEM((ny, rows, K), f32),
        ] + [pltpu.VMEM((n, srows, K), f32) for _ in range(2) for n in (ny, nx, nz)] + [
            pltpu.VMEM((2, 3, srows, K), f32),
            pltpu.SemaphoreType.DMA((STEPS + 1, 6)),
            pltpu.SemaphoreType.DMA((STEPS + 1, 6)),
            pltpu.SemaphoreType.DMA((4, most)),
            pltpu.SemaphoreType.DMA((4, most)),
            pltpu.SemaphoreType.DMA((2, 3, most)),
            pltpu.SemaphoreType.DMA((2, 3, most)),
        ],
        compiler_params=pltpu.CompilerParams(
            collective_id=0, has_side_effects=True, vmem_limit_bytes=48 * 1024 * 1024),
        cost_estimate=pl.CostEstimate(flops=1000000000, bytes_accessed=3000000, transcendentals=0),
    )(basis, modal_now, modal_prev, material_ids, moduli, drive_mask, drive)


def solution(mesh):
    sizes = tuple(mesh.shape[axis] for axis in AXES)
    in_specs = (
        P("gx", None, "gy", "gz", None),
        P(),
        P(),
        P("gx", "gy", "gz"),
        P(),
        P(None, "gx", "gy", "gz"),
        P(),
    )
    out_specs = (P(None, None, "gx", "gy", "gz"), P(None, None, "gx", "gy", "gz"), P(), P())
    return jax.shard_map(functools.partial(shards, sizes), mesh=mesh, in_specs=in_specs,
                         out_specs=out_specs, check_vma=False)
```

```python
import functools
import jax
import jax.numpy as jnp
from jax import lax
from jax.experimental import pallas as pl
from jax.experimental.pallas import tpu as pltpu
from jax.sharding import PartitionSpec as P

STEPS = 4
MESH_IDS = pl.DeviceIdType.MESH
AXES = ("gx", "gy", "gz")
HIGHEST = lax.Precision.HIGHEST
NT = (((1,), (1,)), ((), ()))
NN = (((1,), (0,)), ((), ()))
TN = (((0,), (0,)), ((), ()))

step_squared = 0.1
ramp_steps = 4.0


def dot32(a, b, dims):
    return lax.dot_general(a, b, dims, precision=HIGHEST, preferred_element_type=jnp.float32)


def dot16(a, b, dims):
    return lax.dot_general(a, b, dims, preferred_element_type=jnp.float32)


def small_product(a, b):
    total = a[:, :, 0:1] * b[:, 0:1, :]
    for k in range(1, b.shape[1]):
        total = total + a[:, :, k : k + 1] * b[:, k : k + 1, :]
    return total


def factor(gram):
    s, n, _ = gram.shape
    rows = lax.broadcasted_iota(jnp.int32, (s, n, 128), 1)
    lanes = lax.broadcasted_iota(jnp.int32, (s, n, 128), 2)
    work = jnp.concatenate([gram, jnp.zeros((s, n, 128 - n), jnp.float32)], axis=2)
    work = jnp.where(lanes == rows + n, 1.0, work)
    pivots = jnp.ones((s, n, 128), jnp.float32)
    for k in range(n):
        pivot = work[:, k : k + 1, k : k + 1]
        pivots = jnp.where(rows == k, pivot, pivots)
        if k < n - 1:
            ratio = jnp.where(rows > k, work[:, :, k : k + 1] / pivot, 0.0)
            work = work - ratio * work[:, k : k + 1, :]
    work = work * lax.rsqrt(pivots)
    upper = jnp.where(lanes >= rows, work, 0.0)[:, :, :n]
    return upper, work[:, :, n : 2 * n]


def kernel(sizes, basis_hbm, both_hbm, ids_hbm, moduli_hbm, mask_hbm, drive_hbm,
           disp_out, modes_out, coef_out, rfac_out,
           disp_ref, modes_ref, coef_ref, rfac_ref, out_sem,
           basis_ref, both_ref, ids_ref, moduli_ref, mask_ref, drive_ref, in_sem,
           field_ref, ids_field_ref, hx_ref, hy_ref, hz_ref, zs_ref,
           ix_ref, iy_ref, iz_ref, izs_ref, coup_ref,
           gpart_ref, gy_buf, gx_buf, gz_buf, gslice_ref, gfull_ref,
           early_a, early_b, late_a, late_b, early_out, late_out,
           halo_send, halo_recv, g_send, g_recv, s_send, s_recv):
    nx, ny, nz = sizes
    count = dict(zip(AXES, sizes))
    me = {axis: lax.axis_index(axis) for axis in AXES}
    X, C, Y, Z, K = basis_ref.shape
    J = both_ref.shape[0] // 2
    tiles = X * C * Y
    weight = 1.0 / (tiles * Z * nx * ny * nz)

    loads = [pltpu.make_async_copy(src, dst, in_sem.at[i]) for i, (src, dst) in enumerate((
        (ids_hbm, ids_ref), (both_hbm, both_ref), (basis_hbm, basis_ref),
        (moduli_hbm, moduli_ref), (mask_hbm, mask_ref), (drive_hbm, drive_ref)))]
    for load in loads:
        load.start()

    for ref in (hx_ref, hy_ref, hz_ref, ix_ref, iy_ref, iz_ref):
        ref[...] = jnp.zeros_like(ref)

    plane = [(dx, dy) for dx in range(nx) for dy in range(ny) if dx or dy]

    def plane_peer(dx, dy):
        return {"gx": lax.rem(me["gx"] + dx, nx), "gy": lax.rem(me["gy"] + dy, ny)}

    barrier = pltpu.get_barrier_semaphore()
    for dx, dy in plane:
        pl.semaphore_signal(barrier, inc=1, device_id=plane_peer(dx, dy), device_id_type=MESH_IDS)
    for d in range(1, nz):
        pl.semaphore_signal(barrier, inc=1, device_id={"gz": lax.rem(me["gz"] + d, nz)},
                            device_id_type=MESH_IDS)
    pl.semaphore_wait(barrier, nx * ny + nz - 2)

    def halo_copies(slot, src, zsrc, dst_x, dst_y, dst_z):
        plan = []
        faces = {
            "gx": (src.at[X - 1], src.at[0], dst_x),
            "gy": (src.at[:, Y - 1], src.at[:, 0], dst_y),
            "gz": (zsrc.at[1], zsrc.at[0], dst_z),
        }
        for n_axis, axis in enumerate(AXES):
            up, down, dst = faces[axis]
            for side, face in ((0, up), (1, down)):
                target = me[axis] + (1 if side == 0 else -1)
                copy = pltpu.make_async_remote_copy(
                    src_ref=face, dst_ref=dst.at[side],
                    send_sem=halo_send.at[slot, 2 * n_axis + side],
                    recv_sem=halo_recv.at[slot, 2 * n_axis + side],
                    device_id={axis: target}, device_id_type=MESH_IDS)
                has_target = (me[axis] < count[axis] - 1) if side == 0 else (me[axis] > 0)
                has_source = (me[axis] > 0) if side == 0 else (me[axis] < count[axis] - 1)
                plan.append((has_target, has_source, copy))
        return plan

    def send_all(plan):
        for has_target, _, copy in plan:
            @pl.when(has_target)
            def _(copy=copy):
                copy.start()

    def recv_all(plan):
        for _, has_source, copy in plan:
            @pl.when(has_source)
            def _(copy=copy):
                copy.wait_recv()

    def drain(plan):
        for has_target, _, copy in plan:
            @pl.when(has_target)
            def _(copy=copy):
                copy.wait_send()

    def z_faces(value, zdst):
        turned = value.reshape(-1, Z).T
        zdst[0] = turned[0:8]
        zdst[1] = turned[Z - 8 : Z]

    def neighbours(value, hx, hy, hz):
        shape = value.shape
        x_lo = jnp.concatenate([hx[0][None], value[:-1]], axis=0)
        x_hi = jnp.concatenate([value[1:], hx[1][None]], axis=0)
        y_lo = jnp.concatenate([hy[0][:, None], value[:, :-1]], axis=1)
        y_hi = jnp.concatenate([value[:, 1:], hy[1][:, None]], axis=1)
        flat = value.reshape(-1, Z)
        lanes = lax.broadcasted_iota(jnp.int32, flat.shape, 1)
        turned = jnp.concatenate(
            [hz[1], jnp.zeros((Z - 16, flat.shape[0]), jnp.float32), hz[0]], axis=0).T
        z_lo = pltpu.roll(jnp.where(lanes == Z - 1, turned, flat), 1, 1)
        z_hi = pltpu.roll(jnp.where(lanes == 0, turned, flat), Z - 1, 1)
        return ((x_lo, x_hi), (y_lo, y_hi), (z_lo.reshape(shape), z_hi.reshape(shape)))

    def start_all(copies):
        for copy in copies:
            copy.start()
        return copies

    def exchange(axis, src_of, dst, send_sem, recv_sem):
        copies = []
        for d in range(1, count[axis]):
            peer = lax.rem(me[axis] + d, count[axis])
            copies.append(pltpu.make_async_remote_copy(
                src_ref=src_of(peer), dst_ref=dst.at[me[axis]],
                send_sem=send_sem.at[d], recv_sem=recv_sem.at[d],
                device_id={axis: peer}, device_id_type=MESH_IDS))
        return start_all(copies)

    def exchange_plane(src, dst, send_sem, recv_sem):
        copies = []
        for i, (dx, dy) in enumerate(plane):
            copies.append(pltpu.make_async_remote_copy(
                src_ref=src, dst_ref=dst.at[me["gx"] * ny + me["gy"]],
                send_sem=send_sem.at[i], recv_sem=recv_sem.at[i],
                device_id=plane_peer(dx, dy), device_id_type=MESH_IDS))
        return start_all(copies)

    def finish(started):
        for copy in started:
            copy.wait_recv()
            copy.wait_send()

    def total_of(buf):
        total = buf[0]
        for i in range(1, buf.shape[0]):
            total = total + buf[i]
        return total

    loads[0].wait()
    idf = (ids_ref[...] + 1).astype(jnp.float32)
    idf = jnp.broadcast_to(idf[:, :, None, :], (X, Y, J, Z))
    ids_field_ref[...] = idf
    z_faces(idf, izs_ref)
    ids_plan = halo_copies(STEPS * C, ids_field_ref, izs_ref, ix_ref, iy_ref, iz_ref)
    send_all(ids_plan)

    loads[1].wait()
    loads[2].wait()
    basis = basis_ref[...].reshape(tiles * Z, K)
    start = dot16(both_ref[...], basis, NT)

    def tile_at(x, c, y):
        t = (x * C + c) * Y + y
        return slice(t * Z, (t + 1) * Z)

    def component(flat, c):
        parts = [flat[:, tile_at(x, c, y)] for x in range(X) for y in range(Y)]
        return jnp.stack(parts).reshape(X, Y, J, Z)

    def as_flat(fields):
        return jnp.concatenate(
            [fields[c][x, y] for x in range(X) for c in range(C) for y in range(Y)], axis=1)

    plans = [[halo_copies(s * C + c, field_ref.at[s + 1, c], zs_ref.at[s, c],
                          hx_ref.at[s, c], hy_ref.at[s, c], hz_ref.at[s, c])
              for c in range(C)] for s in range(STEPS)]

    def publish(step, c, value):
        field_ref[step + 1, c] = value
        if step < STEPS:
            z_faces(value, zs_ref.at[step, c])
            send_all(plans[step][c])

    for c in range(C):
        publish(0, c, component(start[:J], c))
        field_ref[0, c] = component(start[J:], c)

    rows = K // ny
    gpart_ref[...] = dot16(basis, basis, TN).reshape(ny, rows, K)
    gy_buf[me["gy"]] = gpart_ref[me["gy"]]
    g_stage = exchange("gy", lambda p: gpart_ref.at[p], gy_buf, g_send.at[0], g_recv.at[0])

    for load in loads[3:]:
        load.wait()
    recv_all(ids_plan)

    def pick(p, index):
        value = jnp.zeros_like(index)
        for m in range(moduli_ref.shape[1]):
            value = jnp.where(index == float(m + 1), moduli_ref[p, m], value)
        return value

    around = neighbours(idf, ix_ref[...], iy_ref[...], iz_ref[...])
    scale = step_squared * pick(2, idf)
    for p in range(2):
        own = pick(p, idf)
        for a in range(3):
            for side in range(2):
                coup_ref[p, a, side] = 0.5 * scale * (own + pick(p, around[a][side]))
    sub = lax.broadcasted_iota(jnp.int32, (J, Z), 0)
    mask = jnp.stack([mask_ref[:, x, y, :] for x in range(X) for y in range(Y)])
    pushed = scale * mask.astype(jnp.float32).reshape(X, Y, J, Z)
    drives = []
    for c in range(C):
        column = jnp.zeros((J, Z), jnp.float32)
        for j in range(J):
            column = jnp.where(sub == j, drive_ref[c, j], column)
        drives.append(column)

    def advance(step, c):
        recv_all(plans[step][c])
        current = field_ref[step + 1, c]
        around = neighbours(current, hx_ref[step, c], hy_ref[step, c], hz_ref[step, c])
        ramp = min(1.0, (step + 1) / ramp_steps)
        following = 2.0 * current - field_ref[step, c] + pushed * (ramp * drives[c])
        for a in range(3):
            for side in range(2):
                following = following - coup_ref[0 if c == a else 1, a, side] * (current - around[a][side])
        publish(step + 1, c, following)

    def snapshots(first, last, pad):
        parts = [as_flat([field_ref[s + 2, c] for c in range(C)]) for s in range(first, last)]
        parts += [jnp.zeros_like(parts[0])] * pad
        return jnp.concatenate(parts, axis=0).astype(jnp.bfloat16)

    def local_stats(snap, n):
        proj = dot16(snap, basis, NN)[: n * J]
        gram = dot16(snap, snap, NT)
        lanes = lax.broadcasted_iota(jnp.int32, (J, gram.shape[1]), 1)
        side = gram[:J]
        for s in range(1, n):
            side = jnp.where(lanes >= s * J, gram[s * J : (s + 1) * J], side)
        side = jnp.concatenate([side, jnp.zeros((J, K - gram.shape[1]), jnp.float32)], axis=1)
        return jnp.concatenate([proj, side], axis=0) * weight

    def reduce_plane(index, value, out, buf):
        out[0] = value
        buf[me["gx"] * ny + me["gy"]] = value
        return exchange_plane(out.at[0], buf, s_send.at[index, 0], s_recv.at[index, 0])

    def reduce_z(index, started, out, buf, next_buf):
        finish(started)
        value = total_of(buf)
        out[1] = value
        next_buf[me["gz"]] = value
        return exchange("gz", lambda p: out.at[1], next_buf, s_send.at[index, 1], s_recv.at[index, 1])

    for step in range(STEPS):
        for c in range(C):
            advance(step, c)
        if step == 0:
            finish(g_stage)
            gslice_ref[0] = total_of(gy_buf)
            gx_buf[me["gx"]] = gslice_ref[0]
            g_stage = exchange("gx", lambda p: gslice_ref.at[0], gx_buf, g_send.at[1], g_recv.at[1])
        if step == 1:
            finish(g_stage)
            gslice_ref[1] = total_of(gx_buf)
            gz_buf[me["gz"]] = gslice_ref[1]
            g_stage = exchange("gz", lambda p: gslice_ref.at[1], gz_buf, g_send.at[2], g_recv.at[2])
        if step == 2:
            early = reduce_plane(0, local_stats(snapshots(0, 3, 1), 3), early_out, early_a)
            finish(g_stage)
            gslice_ref[2] = total_of(gz_buf) * weight
            gfull_ref[me["gy"]] = gslice_ref[2]
            g_stage = exchange("gy", lambda p: gslice_ref.at[2], gfull_ref, g_send.at[3], g_recv.at[3])

    snap = snapshots(STEPS - 1, STEPS, 1)
    late = reduce_plane(1, local_stats(snap, 1), late_out, late_a)
    early = reduce_z(0, early, early_out, early_a, early_b)
    for x in range(X):
        for c in range(C):
            for y in range(Y):
                disp_ref[c, :, x, y, :] = field_ref[STEPS + 1, c, x, y]
    stores = [pltpu.make_async_copy(src, dst, out_sem.at[i]) for i, (src, dst) in enumerate((
        (disp_ref, disp_out), (modes_ref, modes_out), (coef_ref, coef_out), (rfac_ref, rfac_out)))]
    stores[0].start()
    finish(g_stage)
    gram_basis = gfull_ref[...].reshape(K, K)
    late = reduce_z(1, late, late_out, late_a, late_b)
    finish(early)
    first = total_of(early_b)
    finish(late)
    second = total_of(late_b)

    head = (STEPS - 1) * J
    coef1 = jnp.concatenate([first[:head], second[:J]], axis=0)
    coef1_b = coef1.astype(jnp.bfloat16).astype(jnp.float32)

    def blocks(full):
        return jnp.stack([full[J * s : J * s + J, J * s : J * s + J] for s in range(STEPS)])

    snap_gram = jnp.stack(
        [first[head:, J * s : J * s + J] for s in range(STEPS - 1)] + [second[J:, :J]])
    left = coef1 - dot32(coef1_b, gram_basis, NN)
    gram1 = snap_gram - blocks(dot32(coef1_b, left, NT) + dot32(coef1, coef1_b, NT))
    upper1, inverse1 = factor(gram1)
    coef2 = small_product(inverse1, left.reshape(STEPS, J, K)).reshape(STEPS * J, K)
    coef2_b = coef2.astype(jnp.bfloat16).astype(jnp.float32)
    left2 = coef2 - dot32(coef2_b, gram_basis, NN)
    eye = (lax.broadcasted_iota(jnp.int32, (STEPS, J, J), 1)
           == lax.broadcasted_iota(jnp.int32, (STEPS, J, J), 2)).astype(jnp.float32)
    gram2 = eye - blocks(dot32(coef2_b, left2, NT) + dot32(coef2, coef2_b, NT))
    upper2, inverse2 = factor(gram2)
    rfac_ref[...] = small_product(upper2, upper1)
    for s in range(STEPS):
        coef_ref[s, 0] = coef1[J * s : J * s + J]
        coef_ref[s, 1] = coef2[J * s : J * s + J]

    stores[2].start()
    stores[3].start()

    inv1, inv2 = inverse1[STEPS - 1 :], inverse2[STEPS - 1 :]
    tail = slice(J * (STEPS - 1), J * STEPS)
    mix = small_product(inv1, coef1_b[tail][None]) + coef2_b[tail][None]
    mix = small_product(inv2, mix)[0]
    mix_hi = mix.astype(jnp.bfloat16).astype(jnp.float32)
    parts = jnp.concatenate([mix_hi, mix - mix_hi], axis=0).astype(jnp.bfloat16)
    spread = dot16(parts, basis, NT)
    rounded = snap[:J].astype(jnp.float32)
    modes = small_product(small_product(inv2, inv1), rounded[None])[0]
    modes = modes - (spread[:J] + spread[J:])
    for x in range(X):
        for c in range(C):
            for y in range(Y):
                modes_ref[c, :, x, y, :] = modes[:, tile_at(x, c, y)]

    stores[1].start()
    drain(ids_plan)
    for plan in plans:
        for part in plan:
            drain(part)
    for store in stores:
        store.wait()


def write_out(*refs):
    count = (len(refs) - 1) // 2
    copies = [pltpu.make_async_copy(refs[i], refs[count + i], refs[-1].at[i]) for i in range(count)]
    for copy in copies:
        copy.start()
    for copy in copies:
        copy.wait()


def shards(sizes, basis, modal_now, modal_prev, material_ids, moduli, drive_mask, drive):
    nx, ny, nz = sizes
    X, C, Y, Z, K = basis.shape
    J = modal_now.shape[1]
    f32 = jnp.float32
    hbm = pl.BlockSpec(memory_space=pltpu.HBM)
    rows = K // ny
    most = max(nx * ny, nz)
    both = jnp.concatenate([modal_now.T, modal_prev.T], axis=0)
    shapes = (
        jax.ShapeDtypeStruct((C, J, X, Y, Z), f32),
        jax.ShapeDtypeStruct((C, J, X, Y, Z), f32),
        jax.ShapeDtypeStruct((STEPS, 2, J, K), f32),
        jax.ShapeDtypeStruct((STEPS, J, J), f32),
    )
    results = pl.pallas_call(
        functools.partial(kernel, sizes),
        out_shape=shapes,
        in_specs=[hbm] * 6,
        out_specs=(hbm,) * 4,
        scratch_shapes=[pltpu.VMEM(shape.shape, f32) for shape in shapes] + [
            pltpu.SemaphoreType.DMA((4,)),
            pltpu.VMEM(basis.shape, basis.dtype),
            pltpu.VMEM(both.shape, both.dtype),
            pltpu.VMEM(material_ids.shape, material_ids.dtype),
            pltpu.SMEM(moduli.shape, f32),
            pltpu.VMEM(drive_mask.shape, drive_mask.dtype),
            pltpu.SMEM(drive.shape, f32),
            pltpu.SemaphoreType.DMA((6,)),
            pltpu.VMEM((STEPS + 2, C, X, Y, J, Z), f32),
            pltpu.VMEM((X, Y, J, Z), f32),
            pltpu.VMEM((STEPS, C, 2, Y, J, Z), f32),
            pltpu.VMEM((STEPS, C, 2, X, J, Z), f32),
            pltpu.VMEM((STEPS, C, 2, 8, X * Y * J), f32),
            pltpu.VMEM((STEPS, C, 2, 8, X * Y * J), f32),
            pltpu.VMEM((2, Y, J, Z), f32),
            pltpu.VMEM((2, X, J, Z), f32),
            pltpu.VMEM((2, 8, X * Y * J), f32),
            pltpu.VMEM((2, 8, X * Y * J), f32),
            pltpu.VMEM((2, 3, 2, X, Y, J, Z), f32),
            pltpu.VMEM((ny, rows, K), f32),
            pltpu.VMEM((ny, rows, K), f32),
            pltpu.VMEM((nx, rows, K), f32),
            pltpu.VMEM((nz, rows, K), f32),
            pltpu.VMEM((3, rows, K), f32),
            pltpu.VMEM((ny, rows, K), f32),
            pltpu.VMEM((nx * ny, STEPS * J, K), f32),
            pltpu.VMEM((nz, STEPS * J, K), f32),
            pltpu.VMEM((nx * ny, 2 * J, K), f32),
            pltpu.VMEM((nz, 2 * J, K), f32),
            pltpu.VMEM((2, STEPS * J, K), f32),
            pltpu.VMEM((2, 2 * J, K), f32),
            pltpu.SemaphoreType.DMA((STEPS * C + 1, 6)),
            pltpu.SemaphoreType.DMA((STEPS * C + 1, 6)),
            pltpu.SemaphoreType.DMA((4, max(sizes))),
            pltpu.SemaphoreType.DMA((4, max(sizes))),
            pltpu.SemaphoreType.DMA((2, 2, most)),
            pltpu.SemaphoreType.DMA((2, 2, most)),
        ],
        compiler_params=pltpu.CompilerParams(
            collective_id=0, has_side_effects=True, vmem_limit_bytes=66650000),
        cost_estimate=pl.CostEstimate(flops=1000000000, bytes_accessed=3000000, transcendentals=0),
    )(basis, both, material_ids, moduli, drive_mask, drive)
    disp, modes, coefs, factors = pl.pallas_call(
        write_out,
        out_shape=shapes,
        in_specs=[hbm] * 4,
        out_specs=(hbm,) * 4,
        scratch_shapes=[pltpu.SemaphoreType.DMA((4,))],
    )(*results)
    return disp, modes, jnp.swapaxes(coefs, 2, 3), factors


def solution(mesh):
    sizes = tuple(mesh.shape[axis] for axis in AXES)
    in_specs = (
        P("gx", None, "gy", "gz", None),
        P(),
        P(),
        P("gx", "gy", "gz"),
        P(),
        P(None, "gx", "gy", "gz"),
        P(),
    )
    out_specs = (P(None, None, "gx", "gy", "gz"), P(None, None, "gx", "gy", "gz"), P(), P())
    return jax.shard_map(functools.partial(shards, sizes), mesh=mesh, in_specs=in_specs,
                         out_specs=out_specs, check_vma=False)
```

```python
import functools
import jax
import jax.numpy as jnp
from jax import lax
from jax.experimental import pallas as pl
from jax.experimental.pallas import tpu as pltpu
from jax.sharding import PartitionSpec as P

STEPS = 4
MESH_IDS = pl.DeviceIdType.MESH
AXES = ("gx", "gy", "gz")
NT = (((1,), (1,)), ((), ()))
NN = (((1,), (0,)), ((), ()))
TN = (((0,), (0,)), ((), ()))

step_squared = 0.1
ramp_steps = 4.0


def dot16(a, b, dims):
    return lax.dot_general(a, b, dims, preferred_element_type=jnp.float32)


def small_product(a, b):
    total = a[:, :, 0:1] * b[:, 0:1, :]
    for k in range(1, b.shape[1]):
        total = total + a[:, :, k : k + 1] * b[:, k : k + 1, :]
    return total


def factor(gram):
    s, n, _ = gram.shape
    rows = lax.broadcasted_iota(jnp.int32, (s, n, 128), 1)
    lanes = lax.broadcasted_iota(jnp.int32, (s, n, 128), 2)
    work = jnp.concatenate([gram, jnp.zeros((s, n, 128 - n), jnp.float32)], axis=2)
    work = jnp.where(lanes == rows + n, 1.0, work)
    columns = [jnp.broadcast_to(gram[:, :, j : j + 1], (s, n, 128)) for j in range(n)]
    pivots = jnp.ones((s, n, 128), jnp.float32)
    for k in range(n):
        pivot = columns[k][:, k : k + 1]
        pivots = jnp.where(rows == k, pivot, pivots)
        if k < n - 1:
            ratio = jnp.where(rows > k, columns[k] * (1.0 / pivot), 0.0)
            work = work - ratio * work[:, k : k + 1]
            for j in range(k + 1, n):
                columns[j] = columns[j] - ratio * columns[j][:, k : k + 1]
    work = work * lax.rsqrt(pivots)
    upper = jnp.where(lanes >= rows, work, 0.0)[:, :, :n]
    return upper, work[:, :, n : 2 * n]


def in_parts(value):
    parts = []
    for _ in range(3):
        part = value.astype(jnp.bfloat16)
        parts.append(part)
        value = value - part.astype(jnp.float32)
    return parts


def kernel(sizes, basis_hbm, now_hbm, prev_hbm, ids_hbm, moduli_hbm, mask_hbm, drive_hbm,
           disp_out, modes_out, coef_out, rfac_out,
           disp_ref, modes_ref, coef_ref, rfac_ref, out_sem,
           basis_ref, now_ref, prev_ref, ids_ref, moduli_ref, mask_ref, drive_ref, in_sem,
           field_ref, ids_field_ref, hx_ref, hy_ref, hz_ref, zs_ref,
           ix_ref, iy_ref, iz_ref, izs_ref, coup_ref,
           gpart_ref, gy_buf, gx_buf, gz_buf, gslice_ref, gfull_ref,
           early_a, early_b, late_a, late_b, early_out, late_out,
           halo_send, halo_recv, g_send, g_recv, s_send, s_recv):
    nx, ny, nz = sizes
    count = dict(zip(AXES, sizes))
    me = {axis: lax.axis_index(axis) for axis in AXES}
    X, C, Y, Z, K = basis_ref.shape
    J = now_ref.shape[0]
    tiles = X * C * Y
    weight = 1.0 / (tiles * Z * nx * ny * nz)

    loads = [pltpu.make_async_copy(src, dst, in_sem.at[i]) for i, (src, dst) in enumerate((
        (ids_hbm, ids_ref), (now_hbm, now_ref), (prev_hbm, prev_ref), (basis_hbm, basis_ref),
        (moduli_hbm, moduli_ref), (mask_hbm, mask_ref), (drive_hbm, drive_ref)))]
    for load in loads:
        load.start()

    for ref in (hx_ref, hy_ref, hz_ref, ix_ref, iy_ref, iz_ref):
        ref[...] = jnp.zeros_like(ref)

    plane = [(dx, dy) for dx in range(nx) for dy in range(ny) if dx or dy]

    def plane_peer(dx, dy):
        return {"gx": lax.rem(me["gx"] + dx, nx), "gy": lax.rem(me["gy"] + dy, ny)}

    barrier = pltpu.get_barrier_semaphore()
    for dx, dy in plane:
        pl.semaphore_signal(barrier, inc=1, device_id=plane_peer(dx, dy), device_id_type=MESH_IDS)
    for d in range(1, nz):
        pl.semaphore_signal(barrier, inc=1, device_id={"gz": lax.rem(me["gz"] + d, nz)},
                            device_id_type=MESH_IDS)
    pl.semaphore_wait(barrier, nx * ny + nz - 2)

    def halo_copies(slot, src, zsrc, dst_x, dst_y, dst_z):
        plan = []
        faces = {
            "gx": (src.at[X - 1], src.at[0], dst_x),
            "gy": (src.at[:, Y - 1], src.at[:, 0], dst_y),
            "gz": (zsrc.at[1], zsrc.at[0], dst_z),
        }
        for n_axis, axis in enumerate(AXES):
            up, down, dst = faces[axis]
            for side, face in ((0, up), (1, down)):
                target = me[axis] + (1 if side == 0 else -1)
                copy = pltpu.make_async_remote_copy(
                    src_ref=face, dst_ref=dst.at[side],
                    send_sem=halo_send.at[slot, 2 * n_axis + side],
                    recv_sem=halo_recv.at[slot, 2 * n_axis + side],
                    device_id={axis: target}, device_id_type=MESH_IDS)
                has_target = (me[axis] < count[axis] - 1) if side == 0 else (me[axis] > 0)
                has_source = (me[axis] > 0) if side == 0 else (me[axis] < count[axis] - 1)
                plan.append((has_target, has_source, copy))
        return plan

    def send_all(plan):
        for has_target, _, copy in plan:
            @pl.when(has_target)
            def _(copy=copy):
                copy.start()

    def recv_all(plan):
        for _, has_source, copy in plan:
            @pl.when(has_source)
            def _(copy=copy):
                copy.wait_recv()

    def drain(plan):
        for has_target, _, copy in plan:
            @pl.when(has_target)
            def _(copy=copy):
                copy.wait_send()

    def z_faces(value, zdst):
        turned = value.reshape(-1, Z).T
        zdst[0] = turned[0:8]
        zdst[1] = turned[Z - 8 : Z]

    def neighbours(value, hx, hy, hz):
        shape = value.shape
        x_lo = jnp.concatenate([hx[0][None], value[:-1]], axis=0)
        x_hi = jnp.concatenate([value[1:], hx[1][None]], axis=0)
        y_lo = jnp.concatenate([hy[0][:, None], value[:, :-1]], axis=1)
        y_hi = jnp.concatenate([value[:, 1:], hy[1][:, None]], axis=1)
        flat = value.reshape(-1, Z)
        lanes = lax.broadcasted_iota(jnp.int32, flat.shape, 1)
        turned = jnp.concatenate(
            [hz[1], jnp.zeros((Z - 16, flat.shape[0]), jnp.float32), hz[0]], axis=0).T
        z_lo = pltpu.roll(jnp.where(lanes == Z - 1, turned, flat), 1, 1)
        z_hi = pltpu.roll(jnp.where(lanes == 0, turned, flat), Z - 1, 1)
        return ((x_lo, x_hi), (y_lo, y_hi), (z_lo.reshape(shape), z_hi.reshape(shape)))

    def start_all(copies):
        for copy in copies:
            copy.start()
        return copies

    def exchange(axis, src_of, dst, send_sem, recv_sem):
        copies = []
        for d in range(1, count[axis]):
            peer = lax.rem(me[axis] + d, count[axis])
            copies.append(pltpu.make_async_remote_copy(
                src_ref=src_of(peer), dst_ref=dst.at[me[axis]],
                send_sem=send_sem.at[d], recv_sem=recv_sem.at[d],
                device_id={axis: peer}, device_id_type=MESH_IDS))
        return start_all(copies)

    def exchange_plane(src, dst, send_sem, recv_sem):
        copies = []
        for i, (dx, dy) in enumerate(plane):
            copies.append(pltpu.make_async_remote_copy(
                src_ref=src, dst_ref=dst.at[me["gx"] * ny + me["gy"]],
                send_sem=send_sem.at[i], recv_sem=recv_sem.at[i],
                device_id=plane_peer(dx, dy), device_id_type=MESH_IDS))
        return start_all(copies)

    def finish(started):
        for copy in started:
            copy.wait_recv()
            copy.wait_send()

    def total_of(buf):
        total = buf[0]
        for i in range(1, buf.shape[0]):
            total = total + buf[i]
        return total

    loads[0].wait()
    idf = (ids_ref[...] + 1).astype(jnp.float32)
    idf = jnp.broadcast_to(idf[:, :, None, :], (X, Y, J, Z))
    ids_field_ref[...] = idf
    z_faces(idf, izs_ref)
    ids_plan = halo_copies(STEPS * C, ids_field_ref, izs_ref, ix_ref, iy_ref, iz_ref)
    send_all(ids_plan)

    for load in loads[1:4]:
        load.wait()
    basis = basis_ref[...].reshape(tiles * Z, K)
    both = jnp.concatenate([now_ref[...].astype(jnp.float32), prev_ref[...].astype(jnp.float32)], axis=0)
    start = dot16(both.astype(jnp.bfloat16), basis, NT)

    def tile_at(x, c, y):
        t = (x * C + c) * Y + y
        return slice(t * Z, (t + 1) * Z)

    def component(flat, c):
        parts = [flat[:, tile_at(x, c, y)] for x in range(X) for y in range(Y)]
        return jnp.stack(parts).reshape(X, Y, J, Z)

    def as_flat(fields):
        return jnp.concatenate(
            [fields[c][x, y] for x in range(X) for c in range(C) for y in range(Y)], axis=1)

    plans = [[halo_copies(s * C + c, field_ref.at[s + 1, c], zs_ref.at[s, c],
                          hx_ref.at[s, c], hy_ref.at[s, c], hz_ref.at[s, c])
              for c in range(C)] for s in range(STEPS)]

    def publish(step, c, value):
        field_ref[step + 1, c] = value
        if step < STEPS:
            z_faces(value, zs_ref.at[step, c])
            send_all(plans[step][c])

    for c in range(C):
        publish(0, c, component(start[:J], c))
        field_ref[0, c] = component(start[J:], c)

    rows = K // ny
    gpart_ref[...] = dot16(basis, basis, TN).reshape(ny, rows, K)
    gy_buf[me["gy"]] = gpart_ref[me["gy"]]
    g_stage = exchange("gy", lambda p: gpart_ref.at[p], gy_buf, g_send.at[0], g_recv.at[0])

    for load in loads[4:]:
        load.wait()
    recv_all(ids_plan)

    def pick(p, index):
        value = jnp.zeros_like(index)
        for m in range(moduli_ref.shape[1]):
            value = jnp.where(index == float(m + 1), moduli_ref[p, m], value)
        return value

    around = neighbours(idf, ix_ref[...], iy_ref[...], iz_ref[...])
    scale = step_squared * pick(2, idf)
    for p in range(2):
        own = pick(p, idf)
        for a in range(3):
            for side in range(2):
                coup_ref[p, a, side] = 0.5 * scale * (own + pick(p, around[a][side]))
    sub = lax.broadcasted_iota(jnp.int32, (J, Z), 0)
    mask = jnp.stack([mask_ref[:, x, y, :] for x in range(X) for y in range(Y)])
    pushed = scale * mask.astype(jnp.float32).reshape(X, Y, J, Z)
    drives = []
    for c in range(C):
        column = jnp.zeros((J, Z), jnp.float32)
        for j in range(J):
            column = jnp.where(sub == j, drive_ref[c, j], column)
        drives.append(column)

    def advance(step, c):
        recv_all(plans[step][c])
        current = field_ref[step + 1, c]
        around = neighbours(current, hx_ref[step, c], hy_ref[step, c], hz_ref[step, c])
        ramp = min(1.0, (step + 1) / ramp_steps)
        following = 2.0 * current - field_ref[step, c] + pushed * (ramp * drives[c])
        for a in range(3):
            for side in range(2):
                following = following - coup_ref[0 if c == a else 1, a, side] * (current - around[a][side])
        publish(step + 1, c, following)

    def snapshots(first, last, pad):
        parts = [as_flat([field_ref[s + 2, c] for c in range(C)]) for s in range(first, last)]
        parts += [jnp.zeros_like(parts[0])] * pad
        return jnp.concatenate(parts, axis=0).astype(jnp.bfloat16)

    def local_stats(snap, n):
        proj = dot16(snap, basis, NN)[: n * J]
        gram = dot16(snap, snap, NT)
        lanes = lax.broadcasted_iota(jnp.int32, (J, gram.shape[1]), 1)
        side = gram[:J]
        for s in range(1, n):
            side = jnp.where(lanes >= s * J, gram[s * J : (s + 1) * J], side)
        side = jnp.concatenate([side, jnp.zeros((J, K - gram.shape[1]), jnp.float32)], axis=1)
        return jnp.concatenate([proj, side], axis=0) * weight

    def reduce_plane(index, value, out, buf):
        out[0] = value
        buf[me["gx"] * ny + me["gy"]] = value
        return exchange_plane(out.at[0], buf, s_send.at[index, 0], s_recv.at[index, 0])

    def reduce_z(index, started, out, buf, next_buf):
        finish(started)
        value = total_of(buf)
        out[1] = value
        next_buf[me["gz"]] = value
        return exchange("gz", lambda p: out.at[1], next_buf, s_send.at[index, 1], s_recv.at[index, 1])

    for step in range(STEPS):
        for c in range(C):
            advance(step, c)
        if step == 0:
            finish(g_stage)
            gslice_ref[0] = total_of(gy_buf)
            gx_buf[me["gx"]] = gslice_ref[0]
            g_stage = exchange("gx", lambda p: gslice_ref.at[0], gx_buf, g_send.at[1], g_recv.at[1])
        if step == 1:
            finish(g_stage)
            gslice_ref[1] = total_of(gx_buf)
            gz_buf[me["gz"]] = gslice_ref[1]
            g_stage = exchange("gz", lambda p: gslice_ref.at[1], gz_buf, g_send.at[2], g_recv.at[2])
        if step == 2:
            early = reduce_plane(0, local_stats(snapshots(0, 3, 1), 3), early_out, early_a)
            finish(g_stage)
            gslice_ref[2] = total_of(gz_buf) * weight
            gfull_ref[me["gy"]] = gslice_ref[2]
            g_stage = exchange("gy", lambda p: gslice_ref.at[2], gfull_ref, g_send.at[3], g_recv.at[3])

    snap = snapshots(STEPS - 1, STEPS, 1)
    late = reduce_plane(1, local_stats(snap, 1), late_out, late_a)
    early = reduce_z(0, early, early_out, early_a, early_b)
    for x in range(X):
        for c in range(C):
            for y in range(Y):
                disp_ref[c, :, x, y, :] = field_ref[STEPS + 1, c, x, y]
    stores = [pltpu.make_async_copy(src, dst, out_sem.at[i]) for i, (src, dst) in enumerate((
        (disp_ref, disp_out), (modes_ref, modes_out), (coef_ref, coef_out), (rfac_ref, rfac_out)))]
    stores[0].start()
    finish(g_stage)
    gram_parts = jnp.concatenate(in_parts(gfull_ref[...].reshape(K, K)), axis=0)
    late = reduce_z(1, late, late_out, late_a, late_b)
    finish(early)
    first = total_of(early_b)
    finish(late)
    second = total_of(late_b)

    head = (STEPS - 1) * J
    coef1 = jnp.concatenate([first[:head], second[:J]], axis=0)
    coef1_b = coef1.astype(jnp.bfloat16)
    tail = slice(J * (STEPS - 1), J * STEPS)

    def blocks(full):
        return jnp.stack([full[J * s : J * s + J, J * s : J * s + J] for s in range(STEPS)])

    def less_gram(coef, rounded):
        return coef - dot16(jnp.concatenate([rounded] * 3, axis=1), gram_parts, NN)

    def cross(coef, rounded, left):
        lhs = jnp.concatenate([rounded] * 3 + in_parts(coef), axis=1)
        rhs = jnp.concatenate(in_parts(left) + [rounded] * 3, axis=1)
        return blocks(dot16(lhs, rhs, NT))

    snap_gram = jnp.stack(
        [first[head:, J * s : J * s + J] for s in range(STEPS - 1)] + [second[J:, :J]])
    left = less_gram(coef1, coef1_b)
    gram1 = snap_gram - cross(coef1, coef1_b, left)
    resid = snap[:J].astype(jnp.float32) - dot16(coef1_b[tail], basis, NT)
    upper1, inverse1 = factor(gram1)
    coef2 = small_product(inverse1, left.reshape(STEPS, J, K)).reshape(STEPS * J, K)
    coef2_b = coef2.astype(jnp.bfloat16)
    left2 = less_gram(coef2, coef2_b)
    eye = (lax.broadcasted_iota(jnp.int32, (STEPS, J, J), 1)
           == lax.broadcasted_iota(jnp.int32, (STEPS, J, J), 2)).astype(jnp.float32)
    gram2 = eye - cross(coef2, coef2_b, left2)
    resid2 = small_product(inverse1[STEPS - 1 :], resid[None])[0] - dot16(coef2_b[tail], basis, NT)
    upper2, inverse2 = factor(gram2)
    modes = small_product(inverse2[STEPS - 1 :], resid2[None])[0]
    rfac_ref[...] = small_product(upper2, upper1)
    for s in range(STEPS):
        coef_ref[s, 0] = coef1[J * s : J * s + J]
        coef_ref[s, 1] = coef2[J * s : J * s + J]
    stores[2].start()
    stores[3].start()
    for x in range(X):
        for c in range(C):
            for y in range(Y):
                modes_ref[c, :, x, y, :] = modes[:, tile_at(x, c, y)]

    stores[1].start()
    drain(ids_plan)
    for plan in plans:
        for part in plan:
            drain(part)
    for store in stores:
        store.wait()


def write_out(*refs):
    count = (len(refs) - 2) // 3
    sources, results, staged = (refs[count * i : count * (i + 1)] for i in range(3))
    for ends, sem in ((zip(sources, staged), refs[-2]), (zip(staged, results), refs[-1])):
        copies = [pltpu.make_async_copy(src, dst, sem.at[i]) for i, (src, dst) in enumerate(ends)]
        for copy in copies:
            copy.start()
        for copy in copies:
            copy.wait()


def shards(sizes, basis, modal_now, modal_prev, material_ids, moduli, drive_mask, drive):
    nx, ny, nz = sizes
    X, C, Y, Z, K = basis.shape
    J = modal_now.shape[1]
    f32 = jnp.float32
    hbm = pl.BlockSpec(memory_space=pltpu.HBM)
    rows = K // ny
    most = max(nx * ny, nz)
    now, prev = modal_now.T, modal_prev.T
    shapes = (
        jax.ShapeDtypeStruct((C, J, X, Y, Z), f32),
        jax.ShapeDtypeStruct((C, J, X, Y, Z), f32),
        jax.ShapeDtypeStruct((STEPS, 2, J, K), f32),
        jax.ShapeDtypeStruct((STEPS, J, J), f32),
    )
    results = pl.pallas_call(
        functools.partial(kernel, sizes),
        out_shape=shapes,
        in_specs=[hbm] * 7,
        out_specs=(hbm,) * 4,
        scratch_shapes=[pltpu.VMEM(shape.shape, f32) for shape in shapes] + [
            pltpu.SemaphoreType.DMA((4,)),
            pltpu.VMEM(basis.shape, basis.dtype),
            pltpu.VMEM(now.shape, now.dtype),
            pltpu.VMEM(prev.shape, prev.dtype),
            pltpu.VMEM(material_ids.shape, material_ids.dtype),
            pltpu.SMEM(moduli.shape, f32),
            pltpu.VMEM(drive_mask.shape, drive_mask.dtype),
            pltpu.SMEM(drive.shape, f32),
            pltpu.SemaphoreType.DMA((7,)),
            pltpu.VMEM((STEPS + 2, C, X, Y, J, Z), f32),
            pltpu.VMEM((X, Y, J, Z), f32),
            pltpu.VMEM((STEPS, C, 2, Y, J, Z), f32),
            pltpu.VMEM((STEPS, C, 2, X, J, Z), f32),
            pltpu.VMEM((STEPS, C, 2, 8, X * Y * J), f32),
            pltpu.VMEM((STEPS, C, 2, 8, X * Y * J), f32),
            pltpu.VMEM((2, Y, J, Z), f32),
            pltpu.VMEM((2, X, J, Z), f32),
            pltpu.VMEM((2, 8, X * Y * J), f32),
            pltpu.VMEM((2, 8, X * Y * J), f32),
            pltpu.VMEM((2, 3, 2, X, Y, J, Z), f32),
            pltpu.VMEM((ny, rows, K), f32),
            pltpu.VMEM((ny, rows, K), f32),
            pltpu.VMEM((nx, rows, K), f32),
            pltpu.VMEM((nz, rows, K), f32),
            pltpu.VMEM((3, rows, K), f32),
            pltpu.VMEM((ny, rows, K), f32),
            pltpu.VMEM((nx * ny, STEPS * J, K), f32),
            pltpu.VMEM((nz, STEPS * J, K), f32),
            pltpu.VMEM((nx * ny, 2 * J, K), f32),
            pltpu.VMEM((nz, 2 * J, K), f32),
            pltpu.VMEM((2, STEPS * J, K), f32),
            pltpu.VMEM((2, 2 * J, K), f32),
            pltpu.SemaphoreType.DMA((STEPS * C + 1, 6)),
            pltpu.SemaphoreType.DMA((STEPS * C + 1, 6)),
            pltpu.SemaphoreType.DMA((4, max(sizes))),
            pltpu.SemaphoreType.DMA((4, max(sizes))),
            pltpu.SemaphoreType.DMA((2, 2, most)),
            pltpu.SemaphoreType.DMA((2, 2, most)),
        ],
        compiler_params=pltpu.CompilerParams(
            collective_id=0, has_side_effects=True, vmem_limit_bytes=66650000),
        cost_estimate=pl.CostEstimate(flops=1000000000, bytes_accessed=3000000, transcendentals=0),
    )(basis, now, prev, material_ids, moduli, drive_mask, drive)
    disp, modes, coefs, factors = pl.pallas_call(
        write_out,
        out_shape=shapes,
        in_specs=[hbm] * 4,
        out_specs=(hbm,) * 4,
        scratch_shapes=[pltpu.VMEM(shape.shape, f32) for shape in shapes] + [
            pltpu.SemaphoreType.DMA((4,)), pltpu.SemaphoreType.DMA((4,))],
        compiler_params=pltpu.CompilerParams(vmem_limit_bytes=66650000),
    )(*results)
    return disp, modes, jnp.swapaxes(coefs, 2, 3), factors


def solution(mesh):
    sizes = tuple(mesh.shape[axis] for axis in AXES)
    in_specs = (
        P("gx", None, "gy", "gz", None),
        P(),
        P(),
        P("gx", "gy", "gz"),
        P(),
        P(None, "gx", "gy", "gz"),
        P(),
    )
    out_specs = (P(None, None, "gx", "gy", "gz"), P(None, None, "gx", "gy", "gz"), P(), P())
    return jax.shard_map(functools.partial(shards, sizes), mesh=mesh, in_specs=in_specs,
                         out_specs=out_specs, check_vma=False)
```

```python
import functools
import jax
import jax.numpy as jnp
from jax import lax
from jax.experimental import pallas as pl
from jax.experimental.pallas import tpu as pltpu
from jax.sharding import PartitionSpec as P

STEPS = 4
MESH_IDS = pl.DeviceIdType.MESH
AXES = ("gx", "gy", "gz")
NT = (((1,), (1,)), ((), ()))
NN = (((1,), (0,)), ((), ()))
TN = (((0,), (0,)), ((), ()))

step_squared = 0.1
ramp_steps = 4.0


def dot16(a, b, dims):
    return lax.dot_general(a, b, dims, preferred_element_type=jnp.float32)


def small_product(a, b):
    total = a[:, :, 0:1] * b[:, 0:1, :]
    for k in range(1, b.shape[1]):
        total = total + a[:, :, k : k + 1] * b[:, k : k + 1, :]
    return total


def factor(gram):
    s, n, _ = gram.shape
    rows = lax.broadcasted_iota(jnp.int32, (s, n, 128), 1)
    lanes = lax.broadcasted_iota(jnp.int32, (s, n, 128), 2)
    work = jnp.concatenate([gram, jnp.zeros((s, n, 128 - n), jnp.float32)], axis=2)
    work = jnp.where(lanes == rows + n, 1.0, work)
    columns = [jnp.broadcast_to(gram[:, :, j : j + 1], (s, n, 128)) for j in range(n)]
    pivots = jnp.ones((s, n, 128), jnp.float32)
    for k in range(n):
        pivot = columns[k][:, k : k + 1]
        pivots = jnp.where(rows == k, pivot, pivots)
        if k < n - 1:
            ratio = jnp.where(rows > k, columns[k] * (1.0 / pivot), 0.0)
            work = work - ratio * work[:, k : k + 1]
            for j in range(k + 1, n):
                columns[j] = columns[j] - ratio * columns[j][:, k : k + 1]
    work = work * lax.rsqrt(pivots)
    upper = jnp.where(lanes >= rows, work, 0.0)[:, :, :n]
    return upper, work[:, :, n : 2 * n]


def in_parts(value):
    parts = []
    for _ in range(3):
        part = value.astype(jnp.bfloat16)
        parts.append(part)
        value = value - part.astype(jnp.float32)
    return parts


def kernel(sizes, basis_hbm, now_hbm, prev_hbm, ids_hbm, moduli_hbm, mask_hbm, drive_hbm,
           disp_out, modes_out, coef_out, rfac_out,
           disp_ref, modes_ref, coef_ref, rfac_ref, out_sem,
           basis_ref, now_ref, prev_ref, ids_ref, moduli_ref, mask_ref, drive_ref, in_sem,
           field_ref, ids_field_ref, ids_small_ref, hx_ref, hy_ref, hz_ref, zs_ref,
           ix_ref, iy_ref, iz_ref, izs_ref, coup_ref,
           gpart_ref, gy_buf, gx_buf, gz_buf, gslice_ref, gfull_ref,
           early_a, early_b, late_a, late_b, early_out, late_out,
           halo_send, halo_recv, g_send, g_recv, s_send, s_recv):
    nx, ny, nz = sizes
    count = dict(zip(AXES, sizes))
    me = {axis: lax.axis_index(axis) for axis in AXES}
    X, C, Y, Z, K = basis_ref.shape
    J = now_ref.shape[0]
    tiles = X * C * Y
    weight = 1.0 / (tiles * Z * nx * ny * nz)

    loads = [pltpu.make_async_copy(src, dst, in_sem.at[i]) for i, (src, dst) in enumerate((
        (ids_hbm, ids_ref), (now_hbm, now_ref), (prev_hbm, prev_ref),
        (moduli_hbm, moduli_ref), (mask_hbm, mask_ref), (drive_hbm, drive_ref)))]
    chunks = [pltpu.make_async_copy(basis_hbm.at[:, c], basis_ref.at[:, c], in_sem.at[len(loads) + c])
              for c in range(C)]
    for load in loads[:3] + chunks + loads[3:]:
        load.start()

    for ref in (hx_ref, hy_ref, hz_ref, ix_ref, iy_ref, iz_ref):
        ref[...] = jnp.zeros_like(ref)

    plane = [(dx, dy) for dx in range(nx) for dy in range(ny) if dx or dy]

    def plane_peer(dx, dy):
        return {"gx": lax.rem(me["gx"] + dx, nx), "gy": lax.rem(me["gy"] + dy, ny)}

    barrier = pltpu.get_barrier_semaphore()
    for dx, dy in plane:
        pl.semaphore_signal(barrier, inc=1, device_id=plane_peer(dx, dy), device_id_type=MESH_IDS)
    for d in range(1, nz):
        pl.semaphore_signal(barrier, inc=1, device_id={"gz": lax.rem(me["gz"] + d, nz)},
                            device_id_type=MESH_IDS)
    pl.semaphore_wait(barrier, nx * ny + nz - 2)

    def halo_copies(slot, xsrc, src, zsrc, dst_x, dst_y, dst_z):
        plan = []
        faces = {
            "gx": (xsrc.at[X - 1], xsrc.at[0], dst_x),
            "gy": (src.at[:, Y - 1], src.at[:, 0], dst_y),
            "gz": (zsrc.at[1], zsrc.at[0], dst_z),
        }
        for n_axis, axis in enumerate(AXES):
            up, down, dst = faces[axis]
            for side, face in ((0, up), (1, down)):
                target = me[axis] + (1 if side == 0 else -1)
                copy = pltpu.make_async_remote_copy(
                    src_ref=face, dst_ref=dst.at[side],
                    send_sem=halo_send.at[slot, 2 * n_axis + side],
                    recv_sem=halo_recv.at[slot, 2 * n_axis + side],
                    device_id={axis: target}, device_id_type=MESH_IDS)
                has_target = (me[axis] < count[axis] - 1) if side == 0 else (me[axis] > 0)
                has_source = (me[axis] > 0) if side == 0 else (me[axis] < count[axis] - 1)
                plan.append((has_target, has_source, copy))
        return plan

    def send_all(plan):
        for has_target, _, copy in plan:
            @pl.when(has_target)
            def _(copy=copy):
                copy.start()

    def recv_all(plan):
        for _, has_source, copy in plan:
            @pl.when(has_source)
            def _(copy=copy):
                copy.wait_recv()

    def drain(all_plans):
        for n_copy in range(len(all_plans[0])):
            @pl.when(all_plans[0][n_copy][0])
            def _(n_copy=n_copy):
                for plan in all_plans:
                    plan[n_copy][2].wait_send()

    def z_faces(value, zdst):
        turned = value.reshape(-1, Z).T
        zdst[0] = turned[0:8]
        zdst[1] = turned[Z - 8 : Z]

    def neighbours(value, hx, hy, hz):
        shape = value.shape
        x_lo = jnp.concatenate([hx[0][None], value[:-1]], axis=0)
        x_hi = jnp.concatenate([value[1:], hx[1][None]], axis=0)
        y_lo = jnp.concatenate([hy[0][:, None], value[:, :-1]], axis=1)
        y_hi = jnp.concatenate([value[:, 1:], hy[1][:, None]], axis=1)
        flat = value.reshape(-1, Z)
        lanes = lax.broadcasted_iota(jnp.int32, flat.shape, 1)
        turned = jnp.concatenate(
            [hz[1], jnp.zeros((Z - 16, flat.shape[0]), jnp.float32), hz[0]], axis=0).T
        z_lo = pltpu.roll(jnp.where(lanes == Z - 1, turned, flat), 1, 1)
        z_hi = pltpu.roll(jnp.where(lanes == 0, turned, flat), Z - 1, 1)
        return ((x_lo, x_hi), (y_lo, y_hi), (z_lo.reshape(shape), z_hi.reshape(shape)))

    def start_all(copies):
        for copy in copies:
            copy.start()
        return copies

    def exchange(axis, src_of, dst, send_sem, recv_sem):
        copies = []
        for d in range(1, count[axis]):
            peer = lax.rem(me[axis] + d, count[axis])
            copies.append(pltpu.make_async_remote_copy(
                src_ref=src_of(peer), dst_ref=dst.at[me[axis]],
                send_sem=send_sem.at[d], recv_sem=recv_sem.at[d],
                device_id={axis: peer}, device_id_type=MESH_IDS))
        return start_all(copies)

    def exchange_plane(src, dst, send_sem, recv_sem):
        copies = []
        for i, (dx, dy) in enumerate(plane):
            copies.append(pltpu.make_async_remote_copy(
                src_ref=src, dst_ref=dst.at[me["gx"] * ny + me["gy"]],
                send_sem=send_sem.at[i], recv_sem=recv_sem.at[i],
                device_id=plane_peer(dx, dy), device_id_type=MESH_IDS))
        return start_all(copies)

    def finish(started):
        for copy in started:
            copy.wait_recv()
            copy.wait_send()

    def total_of(buf):
        total = buf[0]
        for i in range(1, buf.shape[0]):
            total = total + buf[i]
        return total

    loads[0].wait()
    idf = (ids_ref[...] + 1).astype(jnp.float32)
    ids_small_ref[...] = idf
    idf = jnp.broadcast_to(idf[:, :, None, :], (X, Y, J, Z))
    ids_field_ref[...] = idf
    z_faces(idf, izs_ref)
    ids_plan = halo_copies(STEPS * C, ids_small_ref, ids_field_ref, izs_ref, ix_ref, iy_ref, iz_ref)
    send_all(ids_plan)

    for load in loads[1:3]:
        load.wait()
    both = jnp.concatenate([now_ref[...].astype(jnp.float32), prev_ref[...].astype(jnp.float32)], axis=0)
    both = both.astype(jnp.bfloat16)

    def tile_at(x, c, y):
        t = (x * C + c) * Y + y
        return slice(t * Z, (t + 1) * Z)

    def component(flat):
        parts = [flat[:, t * Z : (t + 1) * Z] for t in range(X * Y)]
        return jnp.stack(parts).reshape(X, Y, J, Z)

    def part_flat(field):
        return jnp.concatenate([field[x, y] for x in range(X) for y in range(Y)], axis=1)

    def as_flat(fields):
        return jnp.concatenate(
            [fields[c][x, y] for x in range(X) for c in range(C) for y in range(Y)], axis=1)

    plans = [[halo_copies(s * C + c, field_ref.at[s + 1, c], field_ref.at[s + 1, c], zs_ref.at[s, c],
                          hx_ref.at[s, c], hy_ref.at[s, c], hz_ref.at[s, c])
              for c in range(C)] for s in range(STEPS)]

    def publish(step, c, value):
        field_ref[step + 1, c] = value
        if step < STEPS:
            z_faces(value, zs_ref.at[step, c])
            send_all(plans[step][c])

    for c in range(C):
        chunks[c].wait()
        start = dot16(both, basis_ref[:, c].reshape(X * Y * Z, K), NT)
        publish(0, c, component(start[:J]))
        field_ref[0, c] = component(start[J:])
    basis = basis_ref[...].reshape(tiles * Z, K)

    rows = K // ny
    gpart_ref[...] = dot16(basis, basis, TN).reshape(ny, rows, K)
    gy_buf[me["gy"]] = gpart_ref[me["gy"]]
    g_stage = exchange("gy", lambda p: gpart_ref.at[p], gy_buf, g_send.at[0], g_recv.at[0])

    for load in loads[3:]:
        load.wait()
    recv_all(ids_plan)

    def pick(p, index):
        value = jnp.zeros_like(index)
        for m in range(moduli_ref.shape[1]):
            value = jnp.where(index == float(m + 1), moduli_ref[p, m], value)
        return value

    side_x = jnp.broadcast_to(ix_ref[...][:, :, None, :], (2, Y, J, Z))
    around = neighbours(idf, side_x, iy_ref[...], iz_ref[...])
    scale = step_squared * pick(2, idf)
    for p in range(2):
        own = pick(p, idf)
        for a in range(3):
            for side in range(2):
                coup_ref[p, a, side] = 0.5 * scale * (own + pick(p, around[a][side]))
    sub = lax.broadcasted_iota(jnp.int32, (J, Z), 0)
    mask = jnp.stack([mask_ref[:, x, y, :] for x in range(X) for y in range(Y)])
    pushed = scale * mask.astype(jnp.float32).reshape(X, Y, J, Z)
    drives = []
    for c in range(C):
        column = jnp.zeros((J, Z), jnp.float32)
        for j in range(J):
            column = jnp.where(sub == j, drive_ref[c, j], column)
        drives.append(column)

    def advance(step, c):
        recv_all(plans[step][c])
        current = field_ref[step + 1, c]
        around = neighbours(current, hx_ref[step, c], hy_ref[step, c], hz_ref[step, c])
        ramp = min(1.0, (step + 1) / ramp_steps)
        following = 2.0 * current - field_ref[step, c] + pushed * (ramp * drives[c])
        for a in range(3):
            for side in range(2):
                following = following - coup_ref[0 if c == a else 1, a, side] * (current - around[a][side])
        publish(step + 1, c, following)

    def snapshots(first, last, pad):
        parts = [as_flat([field_ref[s + 2, c] for c in range(C)]) for s in range(first, last)]
        parts += [jnp.zeros_like(parts[0])] * pad
        return jnp.concatenate(parts, axis=0).astype(jnp.bfloat16)

    def local_stats(snap, n):
        return pack_stats(dot16(snap, basis, NN), dot16(snap, snap, NT), n)

    def pack_stats(proj, gram, n):
        proj = proj[: n * J]
        lanes = lax.broadcasted_iota(jnp.int32, (J, gram.shape[1]), 1)
        side = gram[:J]
        for s in range(1, n):
            side = jnp.where(lanes >= s * J, gram[s * J : (s + 1) * J], side)
        side = jnp.concatenate([side, jnp.zeros((J, K - gram.shape[1]), jnp.float32)], axis=1)
        return jnp.concatenate([proj, side], axis=0) * weight

    def reduce_plane(index, value, out, buf):
        out[0] = value
        buf[me["gx"] * ny + me["gy"]] = value
        return exchange_plane(out.at[0], buf, s_send.at[index, 0], s_recv.at[index, 0])

    def reduce_z(index, started, out, buf, next_buf):
        finish(started)
        value = total_of(buf)
        out[1] = value
        next_buf[me["gz"]] = value
        return exchange("gz", lambda p: out.at[1], next_buf, s_send.at[index, 1], s_recv.at[index, 1])

    proj = gram = 0.0
    for step in range(STEPS):
        for c in range(C):
            advance(step, c)
            if step == STEPS - 1:
                part = part_flat(field_ref[STEPS + 1, c])
                part = jnp.concatenate([part, jnp.zeros_like(part)], axis=0).astype(jnp.bfloat16)
                proj = proj + dot16(part, basis_ref[:, c].reshape(X * Y * Z, K), NN)
                gram = gram + dot16(part, part, NT)
        if step == 0:
            finish(g_stage)
            gslice_ref[0] = total_of(gy_buf)
            gx_buf[me["gx"]] = gslice_ref[0]
            g_stage = exchange("gx", lambda p: gslice_ref.at[0], gx_buf, g_send.at[1], g_recv.at[1])
        if step == 1:
            finish(g_stage)
            gslice_ref[1] = total_of(gx_buf)
            gz_buf[me["gz"]] = gslice_ref[1]
            g_stage = exchange("gz", lambda p: gslice_ref.at[1], gz_buf, g_send.at[2], g_recv.at[2])
        if step == 2:
            early = reduce_plane(0, local_stats(snapshots(0, 3, 1), 3), early_out, early_a)
            finish(g_stage)
            gslice_ref[2] = total_of(gz_buf) * weight
            gfull_ref[me["gy"]] = gslice_ref[2]
            g_stage = exchange("gy", lambda p: gslice_ref.at[2], gfull_ref, g_send.at[3], g_recv.at[3])

    late = reduce_plane(1, pack_stats(proj, gram, 1), late_out, late_a)
    early = reduce_z(0, early, early_out, early_a, early_b)
    for x in range(X):
        for c in range(C):
            for y in range(Y):
                disp_ref[c, :, x, y, :] = field_ref[STEPS + 1, c, x, y]
    stores = [pltpu.make_async_copy(src, dst, out_sem.at[i]) for i, (src, dst) in enumerate((
        (disp_ref, disp_out), (modes_ref, modes_out), (coef_ref, coef_out), (rfac_ref, rfac_out)))]
    stores[0].start()
    drain([ids_plan] + [part for plan in plans for part in plan])
    finish(g_stage)
    gram_parts = jnp.concatenate(in_parts(gfull_ref[...].reshape(K, K)), axis=0)
    late = reduce_z(1, late, late_out, late_a, late_b)
    finish(early)
    first = total_of(early_b)
    snap = as_flat([field_ref[STEPS + 1, c] for c in range(C)]).astype(jnp.bfloat16)
    finish(late)
    second = total_of(late_b)

    head = (STEPS - 1) * J
    coef1 = jnp.concatenate([first[:head], second[:J]], axis=0)
    coef1_b = coef1.astype(jnp.bfloat16)
    tail = slice(J * (STEPS - 1), J * STEPS)

    def blocks(full):
        return jnp.stack([full[J * s : J * s + J, J * s : J * s + J] for s in range(STEPS)])

    def less_gram(coef, rounded):
        return coef - dot16(jnp.concatenate([rounded] * 3, axis=1), gram_parts, NN)

    def cross(coef, rounded, left):
        lhs = jnp.concatenate([rounded] * 3 + in_parts(coef), axis=1)
        rhs = jnp.concatenate(in_parts(left) + [rounded] * 3, axis=1)
        return blocks(dot16(lhs, rhs, NT))

    snap_gram = jnp.stack(
        [first[head:, J * s : J * s + J] for s in range(STEPS - 1)] + [second[J:, :J]])
    left = less_gram(coef1, coef1_b)
    gram1 = snap_gram - cross(coef1, coef1_b, left)
    resid = snap.astype(jnp.float32) - dot16(coef1_b[tail], basis, NT)
    upper1, inverse1 = factor(gram1)
    coef2 = small_product(inverse1, left.reshape(STEPS, J, K)).reshape(STEPS * J, K)
    coef2_b = coef2.astype(jnp.bfloat16)
    left2 = less_gram(coef2, coef2_b)
    eye = (lax.broadcasted_iota(jnp.int32, (STEPS, J, J), 1)
           == lax.broadcasted_iota(jnp.int32, (STEPS, J, J), 2)).astype(jnp.float32)
    gram2 = eye - cross(coef2, coef2_b, left2)
    resid2 = small_product(inverse1[STEPS - 1 :], resid[None])[0] - dot16(coef2_b[tail], basis, NT)
    upper2, inverse2 = factor(gram2)
    modes = small_product(inverse2[STEPS - 1 :], resid2[None])[0]
    rfac_ref[...] = small_product(upper2, upper1)
    for s in range(STEPS):
        coef_ref[s, 0] = coef1[J * s : J * s + J]
        coef_ref[s, 1] = coef2[J * s : J * s + J]
    stores[2].start()
    stores[3].start()
    for x in range(X):
        for c in range(C):
            for y in range(Y):
                modes_ref[c, :, x, y, :] = modes[:, tile_at(x, c, y)]

    stores[1].start()
    for store in stores:
        store.wait()


def write_out(*refs):
    count = (len(refs) - 2) // 3
    sources, results, staged = (refs[count * i : count * (i + 1)] for i in range(3))
    for ends, sem in ((zip(sources, staged), refs[-2]), (zip(staged, results), refs[-1])):
        copies = [pltpu.make_async_copy(src, dst, sem.at[i]) for i, (src, dst) in enumerate(ends)]
        for copy in copies:
            copy.start()
        for copy in copies:
            copy.wait()


def shards(sizes, basis, modal_now, modal_prev, material_ids, moduli, drive_mask, drive):
    nx, ny, nz = sizes
    X, C, Y, Z, K = basis.shape
    J = modal_now.shape[1]
    f32 = jnp.float32
    hbm = pl.BlockSpec(memory_space=pltpu.HBM)
    rows = K // ny
    most = max(nx * ny, nz)
    now, prev = modal_now.T, modal_prev.T
    shapes = (
        jax.ShapeDtypeStruct((C, J, X, Y, Z), f32),
        jax.ShapeDtypeStruct((C, J, X, Y, Z), f32),
        jax.ShapeDtypeStruct((STEPS, 2, J, K), f32),
        jax.ShapeDtypeStruct((STEPS, J, J), f32),
    )
    results = pl.pallas_call(
        functools.partial(kernel, sizes),
        out_shape=shapes,
        in_specs=[hbm] * 7,
        out_specs=(hbm,) * 4,
        scratch_shapes=[pltpu.VMEM(shape.shape, f32) for shape in shapes] + [
            pltpu.SemaphoreType.DMA((4,)),
            pltpu.VMEM(basis.shape, basis.dtype),
            pltpu.VMEM(now.shape, now.dtype),
            pltpu.VMEM(prev.shape, prev.dtype),
            pltpu.VMEM(material_ids.shape, material_ids.dtype),
            pltpu.SMEM(moduli.shape, f32),
            pltpu.VMEM(drive_mask.shape, drive_mask.dtype),
            pltpu.SMEM(drive.shape, f32),
            pltpu.SemaphoreType.DMA((6 + C,)),
            pltpu.VMEM((STEPS + 2, C, X, Y, J, Z), f32),
            pltpu.VMEM((X, Y, J, Z), f32),
            pltpu.VMEM((X, Y, Z), f32),
            pltpu.VMEM((STEPS, C, 2, Y, J, Z), f32),
            pltpu.VMEM((STEPS, C, 2, X, J, Z), f32),
            pltpu.VMEM((STEPS, C, 2, 8, X * Y * J), f32),
            pltpu.VMEM((STEPS, C, 2, 8, X * Y * J), f32),
            pltpu.VMEM((2, Y, Z), f32),
            pltpu.VMEM((2, X, J, Z), f32),
            pltpu.VMEM((2, 8, X * Y * J), f32),
            pltpu.VMEM((2, 8, X * Y * J), f32),
            pltpu.VMEM((2, 3, 2, X, Y, J, Z), f32),
            pltpu.VMEM((ny, rows, K), f32),
            pltpu.VMEM((ny, rows, K), f32),
            pltpu.VMEM((nx, rows, K), f32),
            pltpu.VMEM((nz, rows, K), f32),
            pltpu.VMEM((3, rows, K), f32),
            pltpu.VMEM((ny, rows, K), f32),
            pltpu.VMEM((nx * ny, STEPS * J, K), f32),
            pltpu.VMEM((nz, STEPS * J, K), f32),
            pltpu.VMEM((nx * ny, 2 * J, K), f32),
            pltpu.VMEM((nz, 2 * J, K), f32),
            pltpu.VMEM((2, STEPS * J, K), f32),
            pltpu.VMEM((2, 2 * J, K), f32),
            pltpu.SemaphoreType.DMA((STEPS * C + 1, 6)),
            pltpu.SemaphoreType.DMA((STEPS * C + 1, 6)),
            pltpu.SemaphoreType.DMA((4, max(sizes))),
            pltpu.SemaphoreType.DMA((4, max(sizes))),
            pltpu.SemaphoreType.DMA((2, 2, most)),
            pltpu.SemaphoreType.DMA((2, 2, most)),
        ],
        compiler_params=pltpu.CompilerParams(
            collective_id=0, has_side_effects=True, vmem_limit_bytes=66650000),
        cost_estimate=pl.CostEstimate(flops=1000000000, bytes_accessed=3000000, transcendentals=0),
    )(basis, now, prev, material_ids, moduli, drive_mask, drive)
    disp, modes, coefs, factors = pl.pallas_call(
        write_out,
        out_shape=shapes,
        in_specs=[hbm] * 4,
        out_specs=(hbm,) * 4,
        scratch_shapes=[pltpu.VMEM(shape.shape, f32) for shape in shapes] + [
            pltpu.SemaphoreType.DMA((4,)), pltpu.SemaphoreType.DMA((4,))],
        compiler_params=pltpu.CompilerParams(vmem_limit_bytes=66650000),
    )(*results)
    return disp, modes, jnp.swapaxes(coefs, 2, 3), factors


def solution(mesh):
    sizes = tuple(mesh.shape[axis] for axis in AXES)
    in_specs = (
        P("gx", None, "gy", "gz", None),
        P(),
        P(),
        P("gx", "gy", "gz"),
        P(),
        P(None, "gx", "gy", "gz"),
        P(),
    )
    out_specs = (P(None, None, "gx", "gy", "gz"), P(None, None, "gx", "gy", "gz"), P(), P())
    return jax.shard_map(functools.partial(shards, sizes), mesh=mesh, in_specs=in_specs,
                         out_specs=out_specs, check_vma=False)
```

```python
import functools
import jax
import jax.numpy as jnp
from jax import lax
from jax.experimental import pallas as pl
from jax.experimental.pallas import tpu as pltpu
from jax.sharding import PartitionSpec as P

STEPS = 4
MESH_IDS = pl.DeviceIdType.MESH
AXES = ("gx", "gy", "gz")
NT = (((1,), (1,)), ((), ()))
NN = (((1,), (0,)), ((), ()))
TN = (((0,), (0,)), ((), ()))

step_squared = 0.1
ramp_steps = 4.0


def dot16(a, b, dims):
    return lax.dot_general(a, b, dims, preferred_element_type=jnp.float32)


def small_product(a, b):
    total = a[:, :, 0:1] * b[:, 0:1, :]
    for k in range(1, b.shape[1]):
        total = total + a[:, :, k : k + 1] * b[:, k : k + 1, :]
    return total


def factor(gram):
    s, n, _ = gram.shape
    rows = lax.broadcasted_iota(jnp.int32, (s, n, 128), 1)
    lanes = lax.broadcasted_iota(jnp.int32, (s, n, 128), 2)
    work = jnp.concatenate([gram, jnp.zeros((s, n, 128 - n), jnp.float32)], axis=2)
    work = jnp.where(lanes == rows + n, 1.0, work)
    columns = [jnp.broadcast_to(gram[:, :, j : j + 1], (s, n, 128)) for j in range(n)]
    pivots = jnp.ones((s, n, 128), jnp.float32)
    for k in range(n):
        pivot = columns[k][:, k : k + 1]
        pivots = jnp.where(rows == k, pivot, pivots)
        if k < n - 1:
            ratio = jnp.where(rows > k, columns[k] * (1.0 / pivot), 0.0)
            work = work - ratio * work[:, k : k + 1]
            for j in range(k + 1, n):
                columns[j] = columns[j] - ratio * columns[j][:, k : k + 1]
    work = work * lax.rsqrt(pivots)
    upper = jnp.where(lanes >= rows, work, 0.0)[:, :, :n]
    return upper, work[:, :, n : 2 * n]


def in_parts(value):
    parts = []
    for _ in range(3):
        part = value.astype(jnp.bfloat16)
        parts.append(part)
        value = value - part.astype(jnp.float32)
    return parts


def kernel(sizes, basis_hbm, now_hbm, prev_hbm, ids_hbm, moduli_hbm, mask_hbm, drive_hbm,
           disp_out, modes_out, coef_out, rfac_out,
           disp_ref, modes_ref, coef_ref, rfac_ref, out_sem,
           basis_ref, now_ref, prev_ref, ids_ref, moduli_ref, mask_ref, drive_ref, in_sem,
           field_ref, ids_field_ref, ids_small_ref, hx_ref, hy_ref, hz_ref, zs_ref,
           ix_ref, iy_ref, iz_ref, izs_ref, coup_ref,
           gpart_ref, gy_buf, gx_buf, gz_buf, gslice_ref, gfull_ref,
           early_a, early_b, late_a, late_b, early_out, late_out,
           halo_send, halo_recv, g_send, g_recv, s_send, s_recv):
    nx, ny, nz = sizes
    count = dict(zip(AXES, sizes))
    me = {axis: lax.axis_index(axis) for axis in AXES}
    X, C, Y, Z, K = basis_ref.shape
    J = now_ref.shape[0]
    tiles = X * C * Y
    weight = 1.0 / (tiles * Z * nx * ny * nz)

    loads = [pltpu.make_async_copy(src, dst, in_sem.at[i]) for i, (src, dst) in enumerate((
        (ids_hbm, ids_ref), (now_hbm, now_ref), (prev_hbm, prev_ref),
        (moduli_hbm, moduli_ref), (mask_hbm, mask_ref), (drive_hbm, drive_ref)))]
    chunks = [pltpu.make_async_copy(basis_hbm.at[:, c], basis_ref.at[:, c], in_sem.at[len(loads) + c])
              for c in range(C)]
    for load in loads[:3] + chunks + loads[3:]:
        load.start()

    for ref in (hx_ref, hy_ref, hz_ref, ix_ref, iy_ref, iz_ref):
        ref[...] = jnp.zeros_like(ref)

    plane = [(dx, dy) for dx in range(nx) for dy in range(ny) if dx or dy]

    def plane_peer(dx, dy):
        return {"gx": lax.rem(me["gx"] + dx, nx), "gy": lax.rem(me["gy"] + dy, ny)}

    barrier = pltpu.get_barrier_semaphore()
    for dx, dy in plane:
        pl.semaphore_signal(barrier, inc=1, device_id=plane_peer(dx, dy), device_id_type=MESH_IDS)
    for d in range(1, nz):
        pl.semaphore_signal(barrier, inc=1, device_id={"gz": lax.rem(me["gz"] + d, nz)},
                            device_id_type=MESH_IDS)
    pl.semaphore_wait(barrier, nx * ny + nz - 2)

    def halo_copies(slot, xsrc, src, zsrc, dst_x, dst_y, dst_z):
        plan = []
        faces = {
            "gx": (xsrc.at[X - 1], xsrc.at[0], dst_x),
            "gy": (src.at[:, Y - 1], src.at[:, 0], dst_y),
            "gz": (zsrc.at[1], zsrc.at[0], dst_z),
        }
        for n_axis, axis in enumerate(AXES):
            up, down, dst = faces[axis]
            for side, face in ((0, up), (1, down)):
                target = me[axis] + (1 if side == 0 else -1)
                copy = pltpu.make_async_remote_copy(
                    src_ref=face, dst_ref=dst.at[side],
                    send_sem=halo_send.at[slot, 2 * n_axis + side],
                    recv_sem=halo_recv.at[slot, 2 * n_axis + side],
                    device_id={axis: target}, device_id_type=MESH_IDS)
                has_target = (me[axis] < count[axis] - 1) if side == 0 else (me[axis] > 0)
                has_source = (me[axis] > 0) if side == 0 else (me[axis] < count[axis] - 1)
                plan.append((has_target, has_source, copy))
        return plan

    def send_all(plan):
        for has_target, _, copy in plan:
            @pl.when(has_target)
            def _(copy=copy):
                copy.start()

    def recv_all(plan):
        for _, has_source, copy in plan:
            @pl.when(has_source)
            def _(copy=copy):
                copy.wait_recv()

    def drain(all_plans):
        for n_copy in range(len(all_plans[0])):
            @pl.when(all_plans[0][n_copy][0])
            def _(n_copy=n_copy):
                for plan in all_plans:
                    plan[n_copy][2].wait_send()

    def z_faces(value, zdst):
        turned = value.reshape(-1, Z).T
        zdst[0] = turned[0:8]
        zdst[1] = turned[Z - 8 : Z]

    def x_sides(value, hx):
        return (jnp.concatenate([hx[0][None], value[:-1]], axis=0),
                jnp.concatenate([value[1:], hx[1][None]], axis=0))

    def neighbours(value, hx, hy, hz):
        shape = value.shape
        y_lo = jnp.concatenate([hy[0][:, None], value[:, :-1]], axis=1)
        y_hi = jnp.concatenate([value[:, 1:], hy[1][:, None]], axis=1)
        flat = value.reshape(-1, Z)
        lanes = lax.broadcasted_iota(jnp.int32, flat.shape, 1)
        turned = jnp.concatenate(
            [hz[1], jnp.zeros((Z - 16, flat.shape[0]), jnp.float32), hz[0]], axis=0).T
        z_lo = pltpu.roll(jnp.where(lanes == Z - 1, turned, flat), 1, 1)
        z_hi = pltpu.roll(jnp.where(lanes == 0, turned, flat), Z - 1, 1)
        return (hx if hx is None else x_sides(value, hx), (y_lo, y_hi), (z_lo.reshape(shape), z_hi.reshape(shape)))

    def start_all(copies):
        for copy in copies:
            copy.start()
        return copies

    def exchange(axis, src_of, dst, send_sem, recv_sem):
        copies = []
        for d in range(1, count[axis]):
            peer = lax.rem(me[axis] + d, count[axis])
            copies.append(pltpu.make_async_remote_copy(
                src_ref=src_of(peer), dst_ref=dst.at[me[axis]],
                send_sem=send_sem.at[d], recv_sem=recv_sem.at[d],
                device_id={axis: peer}, device_id_type=MESH_IDS))
        return start_all(copies)

    def exchange_plane(src, dst, send_sem, recv_sem):
        copies = []
        for i, (dx, dy) in enumerate(plane):
            copies.append(pltpu.make_async_remote_copy(
                src_ref=src, dst_ref=dst.at[me["gx"] * ny + me["gy"]],
                send_sem=send_sem.at[i], recv_sem=recv_sem.at[i],
                device_id=plane_peer(dx, dy), device_id_type=MESH_IDS))
        return start_all(copies)

    def finish(started):
        for copy in started:
            copy.wait_recv()
            copy.wait_send()

    def total_of(buf):
        total = buf[0]
        for i in range(1, buf.shape[0]):
            total = total + buf[i]
        return total

    loads[0].wait()
    idf = (ids_ref[...] + 1).astype(jnp.float32)
    ids_small_ref[...] = idf
    idf = jnp.broadcast_to(idf[:, :, None, :], (X, Y, J, Z))
    ids_field_ref[...] = idf
    z_faces(idf, izs_ref)
    ids_plan = halo_copies(STEPS * C, ids_small_ref, ids_field_ref, izs_ref, ix_ref, iy_ref, iz_ref)
    send_all(ids_plan)

    for load in loads[1:3]:
        load.wait()
    both = jnp.concatenate([now_ref[...].astype(jnp.float32), prev_ref[...].astype(jnp.float32)], axis=0)
    both = both.astype(jnp.bfloat16)

    def tile_at(x, c, y):
        t = (x * C + c) * Y + y
        return slice(t * Z, (t + 1) * Z)

    def component(flat):
        parts = [flat[:, t * Z : (t + 1) * Z] for t in range(X * Y)]
        return jnp.stack(parts).reshape(X, Y, J, Z)

    def part_flat(field):
        return jnp.concatenate([field[x, y] for x in range(X) for y in range(Y)], axis=1)

    def as_flat(fields):
        return jnp.concatenate(
            [fields[c][x, y] for x in range(X) for c in range(C) for y in range(Y)], axis=1)

    plans = [[halo_copies(s * C + c, field_ref.at[s + 1, c], field_ref.at[s + 1, c], zs_ref.at[s, c],
                          hx_ref.at[s, c], hy_ref.at[s, c], hz_ref.at[s, c])
              for c in range(C)] for s in range(STEPS)]

    def publish(step, c, value):
        field_ref[step + 1, c] = value
        if step < STEPS:
            send_all(plans[step][c][:4])
            z_faces(value, zs_ref.at[step, c])
            send_all(plans[step][c][4:])

    for c in range(C):
        chunks[c].wait()
        start = dot16(both, basis_ref[:, c].reshape(X * Y * Z, K), NT)
        publish(0, c, component(start[:J]))
        field_ref[0, c] = component(start[J:])
    basis = basis_ref[...].reshape(tiles * Z, K)

    rows = K // ny
    gpart_ref[...] = dot16(basis, basis, TN).reshape(ny, rows, K)
    gy_buf[me["gy"]] = gpart_ref[me["gy"]]
    g_stage = exchange("gy", lambda p: gpart_ref.at[p], gy_buf, g_send.at[0], g_recv.at[0])

    for load in loads[3:]:
        load.wait()
    recv_all(ids_plan)

    def pick(p, index):
        value = jnp.zeros_like(index)
        for m in range(moduli_ref.shape[1]):
            value = jnp.where(index == float(m + 1), moduli_ref[p, m], value)
        return value

    side_x = jnp.broadcast_to(ix_ref[...][:, :, None, :], (2, Y, J, Z))
    around = neighbours(idf, side_x, iy_ref[...], iz_ref[...])
    scale = step_squared * pick(2, idf)
    for p in range(2):
        own = pick(p, idf)
        for a in range(3):
            for side in range(2):
                coup_ref[p, a, side] = 0.5 * scale * (own + pick(p, around[a][side]))
    sub = lax.broadcasted_iota(jnp.int32, (J, Z), 0)
    mask = jnp.stack([mask_ref[:, x, y, :] for x in range(X) for y in range(Y)])
    pushed = scale * mask.astype(jnp.float32).reshape(X, Y, J, Z)
    drives = []
    for c in range(C):
        column = jnp.zeros((J, Z), jnp.float32)
        for j in range(J):
            column = jnp.where(sub == j, drive_ref[c, j], column)
        drives.append(column)

    def advance(step, c):
        recv_all(plans[step][c][2:])
        current = field_ref[step + 1, c]
        around = (None,) + neighbours(current, None, hy_ref[step, c], hz_ref[step, c])[1:]
        ramp = min(1.0, (step + 1) / ramp_steps)
        following = 2.0 * current - field_ref[step, c] + pushed * (ramp * drives[c])
        for a in (1, 2, 0):
            if a == 0:
                recv_all(plans[step][c][:2])
                around = (x_sides(current, hx_ref[step, c]),)
            for side in range(2):
                following = following - coup_ref[0 if c == a else 1, a, side] * (current - around[a][side])
        publish(step + 1, c, following)

    def snapshots(first, last, pad):
        parts = [as_flat([field_ref[s + 2, c] for c in range(C)]) for s in range(first, last)]
        parts += [jnp.zeros_like(parts[0])] * pad
        return jnp.concatenate(parts, axis=0).astype(jnp.bfloat16)

    def local_stats(snap, n):
        return pack_stats(dot16(snap, basis, NN), dot16(snap, snap, NT), n)

    def pack_stats(proj, gram, n):
        proj = proj[: n * J]
        lanes = lax.broadcasted_iota(jnp.int32, (J, gram.shape[1]), 1)
        side = gram[:J]
        for s in range(1, n):
            side = jnp.where(lanes >= s * J, gram[s * J : (s + 1) * J], side)
        side = jnp.concatenate([side, jnp.zeros((J, K - gram.shape[1]), jnp.float32)], axis=1)
        return jnp.concatenate([proj, side], axis=0) * weight

    def reduce_plane(index, value, out, buf):
        out[0] = value
        buf[me["gx"] * ny + me["gy"]] = value
        return exchange_plane(out.at[0], buf, s_send.at[index, 0], s_recv.at[index, 0])

    def reduce_z(index, started, out, buf, next_buf):
        finish(started)
        value = total_of(buf)
        out[1] = value
        next_buf[me["gz"]] = value
        return exchange("gz", lambda p: out.at[1], next_buf, s_send.at[index, 1], s_recv.at[index, 1])

    proj = gram = 0.0
    for step in range(STEPS):
        for c in range(C):
            advance(step, c)
            if step == STEPS - 1:
                part = part_flat(field_ref[STEPS + 1, c])
                part = jnp.concatenate([part, jnp.zeros_like(part)], axis=0).astype(jnp.bfloat16)
                proj = proj + dot16(part, basis_ref[:, c].reshape(X * Y * Z, K), NN)
                gram = gram + dot16(part, part, NT)
        if step == 0:
            finish(g_stage)
            gslice_ref[0] = total_of(gy_buf)
            gx_buf[me["gx"]] = gslice_ref[0]
            g_stage = exchange("gx", lambda p: gslice_ref.at[0], gx_buf, g_send.at[1], g_recv.at[1])
        if step == 1:
            finish(g_stage)
            gslice_ref[1] = total_of(gx_buf)
            gz_buf[me["gz"]] = gslice_ref[1]
            g_stage = exchange("gz", lambda p: gslice_ref.at[1], gz_buf, g_send.at[2], g_recv.at[2])
        if step == 2:
            early = reduce_plane(0, local_stats(snapshots(0, 3, 1), 3), early_out, early_a)
            finish(g_stage)
            gslice_ref[2] = total_of(gz_buf) * weight
            gfull_ref[me["gy"]] = gslice_ref[2]
            g_stage = exchange("gy", lambda p: gslice_ref.at[2], gfull_ref, g_send.at[3], g_recv.at[3])

    late = reduce_plane(1, pack_stats(proj, gram, 1), late_out, late_a)
    early = reduce_z(0, early, early_out, early_a, early_b)
    for x in range(X):
        for c in range(C):
            for y in range(Y):
                disp_ref[c, :, x, y, :] = field_ref[STEPS + 1, c, x, y]
    stores = [pltpu.make_async_copy(src, dst, out_sem.at[i]) for i, (src, dst) in enumerate((
        (disp_ref, disp_out), (modes_ref, modes_out), (coef_ref, coef_out), (rfac_ref, rfac_out)))]
    stores[0].start()
    drain([ids_plan] + [part for plan in plans for part in plan])
    finish(g_stage)
    gram_parts = jnp.concatenate(in_parts(gfull_ref[...].reshape(K, K)), axis=0)
    late = reduce_z(1, late, late_out, late_a, late_b)
    finish(early)
    first = total_of(early_b)
    snap = as_flat([field_ref[STEPS + 1, c] for c in range(C)]).astype(jnp.bfloat16)
    finish(late)
    second = total_of(late_b)

    head = (STEPS - 1) * J
    coef1 = jnp.concatenate([first[:head], second[:J]], axis=0)
    coef1_b = coef1.astype(jnp.bfloat16)
    tail = slice(J * (STEPS - 1), J * STEPS)

    def blocks(full):
        return jnp.stack([full[J * s : J * s + J, J * s : J * s + J] for s in range(STEPS)])

    def less_gram(coef, rounded):
        return coef - dot16(jnp.concatenate([rounded] * 3, axis=1), gram_parts, NN)

    def cross(coef, rounded, left):
        lhs = jnp.concatenate([rounded] * 3 + in_parts(coef), axis=1)
        rhs = jnp.concatenate(in_parts(left) + [rounded] * 3, axis=1)
        return blocks(dot16(lhs, rhs, NT))

    snap_gram = jnp.stack(
        [first[head:, J * s : J * s + J] for s in range(STEPS - 1)] + [second[J:, :J]])
    left = less_gram(coef1, coef1_b)
    gram1 = snap_gram - cross(coef1, coef1_b, left)
    resid = snap.astype(jnp.float32) - dot16(coef1_b[tail], basis, NT)
    upper1, inverse1 = factor(gram1)
    coef2 = small_product(inverse1, left.reshape(STEPS, J, K)).reshape(STEPS * J, K)
    coef2_b = coef2.astype(jnp.bfloat16)
    left2 = less_gram(coef2, coef2_b)
    eye = (lax.broadcasted_iota(jnp.int32, (STEPS, J, J), 1)
           == lax.broadcasted_iota(jnp.int32, (STEPS, J, J), 2)).astype(jnp.float32)
    gram2 = eye - cross(coef2, coef2_b, left2)
    resid2 = small_product(inverse1[STEPS - 1 :], resid[None])[0] - dot16(coef2_b[tail], basis, NT)
    upper2, inverse2 = factor(gram2)
    modes = small_product(inverse2[STEPS - 1 :], resid2[None])[0]
    rfac_ref[...] = small_product(upper2, upper1)
    for s in range(STEPS):
        coef_ref[s, 0] = coef1[J * s : J * s + J]
        coef_ref[s, 1] = coef2[J * s : J * s + J]
    stores[2].start()
    stores[3].start()
    for x in range(X):
        for c in range(C):
            for y in range(Y):
                modes_ref[c, :, x, y, :] = modes[:, tile_at(x, c, y)]

    stores[1].start()
    for store in stores:
        store.wait()


def write_out(*refs):
    count = (len(refs) - 2) // 3
    sources, results, staged = (refs[count * i : count * (i + 1)] for i in range(3))
    for ends, sem in ((zip(sources, staged), refs[-2]), (zip(staged, results), refs[-1])):
        copies = [pltpu.make_async_copy(src, dst, sem.at[i]) for i, (src, dst) in enumerate(ends)]
        for copy in copies:
            copy.start()
        for copy in copies:
            copy.wait()


def shards(sizes, basis, modal_now, modal_prev, material_ids, moduli, drive_mask, drive):
    nx, ny, nz = sizes
    X, C, Y, Z, K = basis.shape
    J = modal_now.shape[1]
    f32 = jnp.float32
    hbm = pl.BlockSpec(memory_space=pltpu.HBM)
    rows = K // ny
    most = max(nx * ny, nz)
    now, prev = modal_now.T, modal_prev.T
    shapes = (
        jax.ShapeDtypeStruct((C, J, X, Y, Z), f32),
        jax.ShapeDtypeStruct((C, J, X, Y, Z), f32),
        jax.ShapeDtypeStruct((STEPS, 2, J, K), f32),
        jax.ShapeDtypeStruct((STEPS, J, J), f32),
    )
    results = pl.pallas_call(
        functools.partial(kernel, sizes),
        out_shape=shapes,
        in_specs=[hbm] * 7,
        out_specs=(hbm,) * 4,
        scratch_shapes=[pltpu.VMEM(shape.shape, f32) for shape in shapes] + [
            pltpu.SemaphoreType.DMA((4,)),
            pltpu.VMEM(basis.shape, basis.dtype),
            pltpu.VMEM(now.shape, now.dtype),
            pltpu.VMEM(prev.shape, prev.dtype),
            pltpu.VMEM(material_ids.shape, material_ids.dtype),
            pltpu.SMEM(moduli.shape, f32),
            pltpu.VMEM(drive_mask.shape, drive_mask.dtype),
            pltpu.SMEM(drive.shape, f32),
            pltpu.SemaphoreType.DMA((6 + C,)),
            pltpu.VMEM((STEPS + 2, C, X, Y, J, Z), f32),
            pltpu.VMEM((X, Y, J, Z), f32),
            pltpu.VMEM((X, Y, Z), f32),
            pltpu.VMEM((STEPS, C, 2, Y, J, Z), f32),
            pltpu.VMEM((STEPS, C, 2, X, J, Z), f32),
            pltpu.VMEM((STEPS, C, 2, 8, X * Y * J), f32),
            pltpu.VMEM((STEPS, C, 2, 8, X * Y * J), f32),
            pltpu.VMEM((2, Y, Z), f32),
            pltpu.VMEM((2, X, J, Z), f32),
            pltpu.VMEM((2, 8, X * Y * J), f32),
            pltpu.VMEM((2, 8, X * Y * J), f32),
            pltpu.VMEM((2, 3, 2, X, Y, J, Z), f32),
            pltpu.VMEM((ny, rows, K), f32),
            pltpu.VMEM((ny, rows, K), f32),
            pltpu.VMEM((nx, rows, K), f32),
            pltpu.VMEM((nz, rows, K), f32),
            pltpu.VMEM((3, rows, K), f32),
            pltpu.VMEM((ny, rows, K), f32),
            pltpu.VMEM((nx * ny, STEPS * J, K), f32),
            pltpu.VMEM((nz, STEPS * J, K), f32),
            pltpu.VMEM((nx * ny, 2 * J, K), f32),
            pltpu.VMEM((nz, 2 * J, K), f32),
            pltpu.VMEM((2, STEPS * J, K), f32),
            pltpu.VMEM((2, 2 * J, K), f32),
            pltpu.SemaphoreType.DMA((STEPS * C + 1, 6)),
            pltpu.SemaphoreType.DMA((STEPS * C + 1, 6)),
            pltpu.SemaphoreType.DMA((4, max(sizes))),
            pltpu.SemaphoreType.DMA((4, max(sizes))),
            pltpu.SemaphoreType.DMA((2, 2, most)),
            pltpu.SemaphoreType.DMA((2, 2, most)),
        ],
        compiler_params=pltpu.CompilerParams(
            collective_id=0, has_side_effects=True, vmem_limit_bytes=66650000),
        cost_estimate=pl.CostEstimate(flops=1000000000, bytes_accessed=3000000, transcendentals=0),
    )(basis, now, prev, material_ids, moduli, drive_mask, drive)
    disp, modes, coefs, factors = pl.pallas_call(
        write_out,
        out_shape=shapes,
        in_specs=[hbm] * 4,
        out_specs=(hbm,) * 4,
        scratch_shapes=[pltpu.VMEM(shape.shape, f32) for shape in shapes] + [
            pltpu.SemaphoreType.DMA((4,)), pltpu.SemaphoreType.DMA((4,))],
        compiler_params=pltpu.CompilerParams(vmem_limit_bytes=66650000),
    )(*results)
    return disp, modes, jnp.swapaxes(coefs, 2, 3), factors


def solution(mesh):
    sizes = tuple(mesh.shape[axis] for axis in AXES)
    in_specs = (
        P("gx", None, "gy", "gz", None),
        P(),
        P(),
        P("gx", "gy", "gz"),
        P(),
        P(None, "gx", "gy", "gz"),
        P(),
    )
    out_specs = (P(None, None, "gx", "gy", "gz"), P(None, None, "gx", "gy", "gz"), P(), P())
    return jax.shard_map(functools.partial(shards, sizes), mesh=mesh, in_specs=in_specs,
                         out_specs=out_specs, check_vma=False)
```

```python
import functools
import jax
import jax.numpy as jnp
from jax import lax
from jax.experimental import pallas as pl
from jax.experimental.pallas import tpu as pltpu
from jax.sharding import PartitionSpec as P

STEPS = 4
MESH_IDS = pl.DeviceIdType.MESH
AXES = ("gx", "gy", "gz")
NT = (((1,), (1,)), ((), ()))
NN = (((1,), (0,)), ((), ()))
TN = (((0,), (0,)), ((), ()))

step_squared = 0.1
ramp_steps = 4.0


def dot16(a, b, dims):
    return lax.dot_general(a, b, dims, preferred_element_type=jnp.float32)


def small_product(a, b):
    total = a[:, :, 0:1] * b[:, 0:1, :]
    for k in range(1, b.shape[1]):
        total = total + a[:, :, k : k + 1] * b[:, k : k + 1, :]
    return total


def factor(gram):
    s, n, _ = gram.shape
    rows = lax.broadcasted_iota(jnp.int32, (s, n, 128), 1)
    lanes = lax.broadcasted_iota(jnp.int32, (s, n, 128), 2)
    work = jnp.concatenate([gram, jnp.zeros((s, n, 128 - n), jnp.float32)], axis=2)
    work = jnp.where(lanes == rows + n, 1.0, work)
    columns = [jnp.broadcast_to(gram[:, :, j : j + 1], (s, n, 128)) for j in range(n)]
    pivots = jnp.ones((s, n, 128), jnp.float32)
    for k in range(n):
        pivot = columns[k][:, k : k + 1]
        pivots = jnp.where(rows == k, pivot, pivots)
        if k < n - 1:
            ratio = jnp.where(rows > k, columns[k] * (1.0 / pivot), 0.0)
            work = work - ratio * work[:, k : k + 1]
            for j in range(k + 1, n):
                columns[j] = columns[j] - ratio * columns[j][:, k : k + 1]
    work = work * lax.rsqrt(pivots)
    upper = jnp.where(lanes >= rows, work, 0.0)[:, :, :n]
    return upper, work[:, :, n : 2 * n]


def in_parts(value):
    parts = []
    for _ in range(3):
        part = value.astype(jnp.bfloat16)
        parts.append(part)
        value = value - part.astype(jnp.float32)
    return parts


def kernel(sizes, basis_hbm, now_hbm, prev_hbm, ids_hbm, moduli_hbm, mask_hbm, drive_hbm,
           disp_out, modes_out, coef_out, rfac_out,
           disp_ref, modes_ref, coef_ref, rfac_ref, out_sem,
           basis_ref, now_ref, prev_ref, ids_ref, moduli_ref, mask_ref, drive_ref, in_sem,
           field_ref, ids_field_ref, ids_small_ref, hx_ref, hy_ref, hz_ref, zs_ref,
           ix_ref, iy_ref, iz_ref, izs_ref, coup_ref,
           gpart_ref, gy_buf, gx_buf, gz_buf, gslice_ref, gfull_ref,
           early_a, early_b, late_a, late_b, early_out, late_out,
           halo_send, halo_recv, g_send, g_recv, s_send, s_recv):
    nx, ny, nz = sizes
    count = dict(zip(AXES, sizes))
    me = {axis: lax.axis_index(axis) for axis in AXES}
    X, C, Y, Z, K = basis_ref.shape
    J = now_ref.shape[0]
    tiles = X * C * Y
    weight = 1.0 / (tiles * Z * nx * ny * nz)

    loads = [pltpu.make_async_copy(src, dst, in_sem.at[i]) for i, (src, dst) in enumerate((
        (ids_hbm, ids_ref), (now_hbm, now_ref), (prev_hbm, prev_ref),
        (moduli_hbm, moduli_ref), (mask_hbm, mask_ref), (drive_hbm, drive_ref)))]
    chunks = [pltpu.make_async_copy(basis_hbm.at[:, c], basis_ref.at[:, c], in_sem.at[len(loads) + c])
              for c in range(C)]
    for load in loads[:3] + chunks + loads[3:]:
        load.start()

    for ref in (hx_ref, hy_ref, hz_ref, ix_ref, iy_ref, iz_ref):
        ref[...] = jnp.zeros_like(ref)

    plane = [(dx, dy) for dx in range(nx) for dy in range(ny) if dx or dy]

    def plane_peer(dx, dy):
        return {"gx": lax.rem(me["gx"] + dx, nx), "gy": lax.rem(me["gy"] + dy, ny)}

    barrier = pltpu.get_barrier_semaphore()
    for dx, dy in plane:
        pl.semaphore_signal(barrier, inc=1, device_id=plane_peer(dx, dy), device_id_type=MESH_IDS)
    for d in range(1, nz):
        pl.semaphore_signal(barrier, inc=1, device_id={"gz": lax.rem(me["gz"] + d, nz)},
                            device_id_type=MESH_IDS)
    pl.semaphore_wait(barrier, nx * ny + nz - 2)

    def halo_copies(slot, xsrc, src, zsrc, dst_x, dst_y, dst_z):
        plan = []
        faces = {
            "gx": (xsrc.at[X - 1], xsrc.at[0], dst_x),
            "gy": (src.at[:, Y - 1], src.at[:, 0], dst_y),
            "gz": (zsrc.at[1], zsrc.at[0], dst_z),
        }
        for n_axis, axis in enumerate(AXES):
            up, down, dst = faces[axis]
            for side, face in ((0, up), (1, down)):
                target = me[axis] + (1 if side == 0 else -1)
                copy = pltpu.make_async_remote_copy(
                    src_ref=face, dst_ref=dst.at[side],
                    send_sem=halo_send.at[slot, 2 * n_axis + side],
                    recv_sem=halo_recv.at[slot, 2 * n_axis + side],
                    device_id={axis: target}, device_id_type=MESH_IDS)
                has_target = (me[axis] < count[axis] - 1) if side == 0 else (me[axis] > 0)
                has_source = (me[axis] > 0) if side == 0 else (me[axis] < count[axis] - 1)
                plan.append((has_target, has_source, copy))
        return plan

    def send_all(plan):
        for has_target, _, copy in plan:
            @pl.when(has_target)
            def _(copy=copy):
                copy.start()

    def recv_all(plan):
        for _, has_source, copy in plan:
            @pl.when(has_source)
            def _(copy=copy):
                copy.wait_recv()

    def drain(all_plans):
        for n_copy in range(len(all_plans[0])):
            @pl.when(all_plans[0][n_copy][0])
            def _(n_copy=n_copy):
                for plan in all_plans:
                    plan[n_copy][2].wait_send()

    def z_faces(value, zdst):
        turned = value.reshape(-1, Z).T
        zdst[0] = turned[0:8]
        zdst[1] = turned[Z - 8 : Z]

    def x_sides(value, hx):
        return (jnp.concatenate([hx[0][None], value[:-1]], axis=0),
                jnp.concatenate([value[1:], hx[1][None]], axis=0))

    def neighbours(value, hx, hy, hz):
        shape = value.shape
        y_lo = jnp.concatenate([hy[0][:, None], value[:, :-1]], axis=1)
        y_hi = jnp.concatenate([value[:, 1:], hy[1][:, None]], axis=1)
        flat = value.reshape(-1, Z)
        lanes = lax.broadcasted_iota(jnp.int32, flat.shape, 1)
        turned = jnp.concatenate(
            [hz[1], jnp.zeros((Z - 16, flat.shape[0]), jnp.float32), hz[0]], axis=0).T
        z_lo = pltpu.roll(jnp.where(lanes == Z - 1, turned, flat), 1, 1)
        z_hi = pltpu.roll(jnp.where(lanes == 0, turned, flat), Z - 1, 1)
        return (hx if hx is None else x_sides(value, hx), (y_lo, y_hi), (z_lo.reshape(shape), z_hi.reshape(shape)))

    def start_all(copies):
        for copy in copies:
            copy.start()
        return copies

    def exchange(axis, src_of, dst, send_sem, recv_sem):
        copies = []
        for d in range(1, count[axis]):
            peer = lax.rem(me[axis] + d, count[axis])
            copies.append(pltpu.make_async_remote_copy(
                src_ref=src_of(peer), dst_ref=dst.at[me[axis]],
                send_sem=send_sem.at[d], recv_sem=recv_sem.at[d],
                device_id={axis: peer}, device_id_type=MESH_IDS))
        return start_all(copies)

    def exchange_plane(src, dst, send_sem, recv_sem):
        copies = []
        for i, (dx, dy) in enumerate(plane):
            copies.append(pltpu.make_async_remote_copy(
                src_ref=src, dst_ref=dst.at[me["gx"] * ny + me["gy"]],
                send_sem=send_sem.at[i], recv_sem=recv_sem.at[i],
                device_id=plane_peer(dx, dy), device_id_type=MESH_IDS))
        return start_all(copies)

    def finish(started):
        for copy in started:
            copy.wait_recv()
            copy.wait_send()

    def total_of(buf):
        total = buf[0]
        for i in range(1, buf.shape[0]):
            total = total + buf[i]
        return total

    loads[0].wait()
    idf = (ids_ref[...] + 1).astype(jnp.float32)
    ids_small_ref[...] = idf
    idf = jnp.broadcast_to(idf[:, :, None, :], (X, Y, J, Z))
    ids_field_ref[...] = idf
    z_faces(idf, izs_ref)
    ids_plan = halo_copies(STEPS * C, ids_small_ref, ids_field_ref, izs_ref, ix_ref, iy_ref, iz_ref)
    send_all(ids_plan)

    for load in loads[1:3]:
        load.wait()
    both = jnp.concatenate([now_ref[...].astype(jnp.float32), prev_ref[...].astype(jnp.float32)], axis=0)
    both = both.astype(jnp.bfloat16)

    def tile_at(x, c, y):
        t = (x * C + c) * Y + y
        return slice(t * Z, (t + 1) * Z)

    def component(flat):
        parts = [flat[:, t * Z : (t + 1) * Z] for t in range(X * Y)]
        return jnp.stack(parts).reshape(X, Y, J, Z)

    def part_flat(field):
        return jnp.concatenate([field[x, y] for x in range(X) for y in range(Y)], axis=1)

    def as_flat(fields):
        return jnp.concatenate(
            [fields[c][x, y] for x in range(X) for c in range(C) for y in range(Y)], axis=1)

    plans = [[halo_copies(s * C + c, field_ref.at[s + 1, c], field_ref.at[s + 1, c], zs_ref.at[s, c],
                          hx_ref.at[s, c], hy_ref.at[s, c], hz_ref.at[s, c])
              for c in range(C)] for s in range(STEPS)]

    def publish(step, c, value):
        field_ref[step + 1, c] = value
        if step < STEPS:
            send_all(plans[step][c][:4])
            z_faces(value, zs_ref.at[step, c])
            send_all(plans[step][c][4:])

    for c in range(C):
        chunks[c].wait()
        start = dot16(both, basis_ref[:, c].reshape(X * Y * Z, K), NT)
        publish(0, c, component(start[:J]))
        field_ref[0, c] = component(start[J:])
    basis = basis_ref[...].reshape(tiles * Z, K)

    rows = K // ny
    gpart_ref[...] = dot16(basis, basis, TN).reshape(ny, rows, K)
    gy_buf[me["gy"]] = gpart_ref[me["gy"]]
    g_stage = exchange("gy", lambda p: gpart_ref.at[p], gy_buf, g_send.at[0], g_recv.at[0])

    for load in loads[3:]:
        load.wait()
    recv_all(ids_plan)

    def pick(p, index):
        value = jnp.zeros_like(index)
        for m in range(moduli_ref.shape[1]):
            value = jnp.where(index == float(m + 1), moduli_ref[p, m], value)
        return value

    side_x = jnp.broadcast_to(ix_ref[...][:, :, None, :], (2, Y, J, Z))
    around = neighbours(idf, side_x, iy_ref[...], iz_ref[...])
    scale = step_squared * pick(2, idf)
    for p in range(2):
        own = pick(p, idf)
        for a in range(3):
            for side in range(2):
                coup_ref[p, a, side] = 0.5 * scale * (own + pick(p, around[a][side]))
    sub = lax.broadcasted_iota(jnp.int32, (J, Z), 0)
    mask = jnp.stack([mask_ref[:, x, y, :] for x in range(X) for y in range(Y)])
    pushed = scale * mask.astype(jnp.float32).reshape(X, Y, J, Z)
    drives = []
    for c in range(C):
        column = jnp.zeros((J, Z), jnp.float32)
        for j in range(J):
            column = jnp.where(sub == j, drive_ref[c, j], column)
        drives.append(column)

    def advance(step, c):
        recv_all(plans[step][c][2:])
        current = field_ref[step + 1, c]
        around = (None,) + neighbours(current, None, hy_ref[step, c], hz_ref[step, c])[1:]
        ramp = min(1.0, (step + 1) / ramp_steps)
        following = 2.0 * current - field_ref[step, c] + pushed * (ramp * drives[c])
        for a in (1, 2, 0):
            if a == 0:
                recv_all(plans[step][c][:2])
                around = (x_sides(current, hx_ref[step, c]),)
            for side in range(2):
                following = following - coup_ref[0 if c == a else 1, a, side] * (current - around[a][side])
        publish(step + 1, c, following)

    def snapshots(first, last, pad):
        parts = [as_flat([field_ref[s + 2, c] for c in range(C)]) for s in range(first, last)]
        parts += [jnp.zeros_like(parts[0])] * pad
        return jnp.concatenate(parts, axis=0).astype(jnp.bfloat16)

    def local_stats(snap, n):
        return pack_stats(dot16(snap, basis, NN), dot16(snap, snap, NT), n)

    def pack_stats(proj, gram, n):
        proj = proj[: n * J]
        lanes = lax.broadcasted_iota(jnp.int32, (J, gram.shape[1]), 1)
        side = gram[:J]
        for s in range(1, n):
            side = jnp.where(lanes >= s * J, gram[s * J : (s + 1) * J], side)
        side = jnp.concatenate([side, jnp.zeros((J, K - gram.shape[1]), jnp.float32)], axis=1)
        return jnp.concatenate([proj, side], axis=0) * weight

    def reduce_plane(index, value, out, buf):
        out[0] = value
        buf[me["gx"] * ny + me["gy"]] = value
        return exchange_plane(out.at[0], buf, s_send.at[index, 0], s_recv.at[index, 0])

    def reduce_z(index, started, out, buf, next_buf):
        finish(started)
        value = total_of(buf)
        out[1] = value
        next_buf[me["gz"]] = value
        return exchange("gz", lambda p: out.at[1], next_buf, s_send.at[index, 1], s_recv.at[index, 1])

    proj = gram = 0.0
    for step in range(STEPS):
        for c in range(C):
            advance(step, c)
            if step == STEPS - 1:
                part = part_flat(field_ref[STEPS + 1, c])
                part = jnp.concatenate([part, jnp.zeros_like(part)], axis=0).astype(jnp.bfloat16)
                proj = proj + dot16(part, basis_ref[:, c].reshape(X * Y * Z, K), NN)
                gram = gram + dot16(part, part, NT)
        if step == 0:
            finish(g_stage)
            gslice_ref[0] = total_of(gy_buf)
            gx_buf[me["gx"]] = gslice_ref[0]
            g_stage = exchange("gx", lambda p: gslice_ref.at[0], gx_buf, g_send.at[1], g_recv.at[1])
        if step == 1:
            finish(g_stage)
            gslice_ref[1] = total_of(gx_buf)
            gz_buf[me["gz"]] = gslice_ref[1]
            g_stage = exchange("gz", lambda p: gslice_ref.at[1], gz_buf, g_send.at[2], g_recv.at[2])
        if step == 2:
            early = reduce_plane(0, local_stats(snapshots(0, 3, 1), 3), early_out, early_a)
            finish(g_stage)
            gslice_ref[2] = total_of(gz_buf) * weight
            gfull_ref[me["gy"]] = gslice_ref[2]
            g_stage = exchange("gy", lambda p: gslice_ref.at[2], gfull_ref, g_send.at[3], g_recv.at[3])

    late = reduce_plane(1, pack_stats(proj, gram, 1), late_out, late_a)
    early = reduce_z(0, early, early_out, early_a, early_b)
    for x in range(X):
        for c in range(C):
            for y in range(Y):
                disp_ref[c, :, x, y, :] = field_ref[STEPS + 1, c, x, y]
    stores = [pltpu.make_async_copy(src, dst, out_sem.at[i]) for i, (src, dst) in enumerate((
        (disp_ref, disp_out), (modes_ref, modes_out), (coef_ref, coef_out), (rfac_ref, rfac_out)))]
    stores[0].start()
    drain([ids_plan] + [part for plan in plans for part in plan])
    finish(g_stage)
    gram_parts = jnp.concatenate(in_parts(gfull_ref[...].reshape(K, K)), axis=0)
    late = reduce_z(1, late, late_out, late_a, late_b)
    finish(early)
    first = total_of(early_b)
    snap = as_flat([field_ref[STEPS + 1, c] for c in range(C)]).astype(jnp.bfloat16)
    finish(late)
    second = total_of(late_b)

    head = (STEPS - 1) * J
    coef1 = jnp.concatenate([first[:head], second[:J]], axis=0)
    coef1_b = coef1.astype(jnp.bfloat16)
    tail = slice(J * (STEPS - 1), J * STEPS)

    def blocks(full):
        return jnp.stack([full[J * s : J * s + J, J * s : J * s + J] for s in range(STEPS)])

    def less_gram(coef, rounded):
        return coef - dot16(jnp.concatenate([rounded] * 3, axis=1), gram_parts, NN)

    def cross(coef, rounded, left):
        lhs = jnp.concatenate([rounded] * 3 + in_parts(coef), axis=1)
        rhs = jnp.concatenate(in_parts(left) + [rounded] * 3, axis=1)
        return blocks(dot16(lhs, rhs, NT))

    snap_gram = jnp.stack(
        [first[head:, J * s : J * s + J] for s in range(STEPS - 1)] + [second[J:, :J]])
    left = less_gram(coef1, coef1_b)
    gram1 = snap_gram - cross(coef1, coef1_b, left)
    resid = snap.astype(jnp.float32) - dot16(coef1_b[tail], basis, NT)
    upper1, inverse1 = factor(gram1)
    coef2 = small_product(inverse1, left.reshape(STEPS, J, K)).reshape(STEPS * J, K)
    coef2_b = coef2.astype(jnp.bfloat16)
    left2 = less_gram(coef2, coef2_b)
    eye = (lax.broadcasted_iota(jnp.int32, (STEPS, J, J), 1)
           == lax.broadcasted_iota(jnp.int32, (STEPS, J, J), 2)).astype(jnp.float32)
    gram2 = eye - cross(coef2, coef2_b, left2)
    resid2 = small_product(inverse1[STEPS - 1 :], resid[None])[0] - dot16(coef2_b[tail], basis, NT)
    upper2, inverse2 = factor(gram2)
    modes = small_product(inverse2[STEPS - 1 :], resid2[None])[0]
    rfac_ref[...] = small_product(upper2, upper1)
    for s in range(STEPS):
        coef_ref[s, 0] = coef1[J * s : J * s + J]
        coef_ref[s, 1] = coef2[J * s : J * s + J]
    stores[2].start()
    stores[3].start()
    for x in range(X):
        for c in range(C):
            for y in range(Y):
                modes_ref[c, :, x, y, :] = modes[:, tile_at(x, c, y)]

    stores[1].start()
    for store in stores:
        store.wait()


def write_out(*refs):
    count = (len(refs) - 2) // 3
    sources, results, staged = (refs[count * i : count * (i + 1)] for i in range(3))
    ins = [pltpu.make_async_copy(sources[i], staged[i], refs[-2].at[i]) for i in range(count)]
    outs = [pltpu.make_async_copy(staged[i], results[i], refs[-1].at[i]) for i in range(count)]
    for copy in ins:
        copy.start()
    for arrived, copy in zip(ins, outs):
        arrived.wait()
        copy.start()
    for copy in outs:
        copy.wait()


def shards(sizes, basis, modal_now, modal_prev, material_ids, moduli, drive_mask, drive):
    nx, ny, nz = sizes
    X, C, Y, Z, K = basis.shape
    J = modal_now.shape[1]
    f32 = jnp.float32
    hbm = pl.BlockSpec(memory_space=pltpu.HBM)
    rows = K // ny
    most = max(nx * ny, nz)
    now, prev = modal_now.T, modal_prev.T
    shapes = (
        jax.ShapeDtypeStruct((C, J, X, Y, Z), f32),
        jax.ShapeDtypeStruct((C, J, X, Y, Z), f32),
        jax.ShapeDtypeStruct((STEPS, 2, J, K), f32),
        jax.ShapeDtypeStruct((STEPS, J, J), f32),
    )
    results = pl.pallas_call(
        functools.partial(kernel, sizes),
        out_shape=shapes,
        in_specs=[hbm] * 7,
        out_specs=(hbm,) * 4,
        scratch_shapes=[pltpu.VMEM(shape.shape, f32) for shape in shapes] + [
            pltpu.SemaphoreType.DMA((4,)),
            pltpu.VMEM(basis.shape, basis.dtype),
            pltpu.VMEM(now.shape, now.dtype),
            pltpu.VMEM(prev.shape, prev.dtype),
            pltpu.VMEM(material_ids.shape, material_ids.dtype),
            pltpu.SMEM(moduli.shape, f32),
            pltpu.VMEM(drive_mask.shape, drive_mask.dtype),
            pltpu.SMEM(drive.shape, f32),
            pltpu.SemaphoreType.DMA((6 + C,)),
            pltpu.VMEM((STEPS + 2, C, X, Y, J, Z), f32),
            pltpu.VMEM((X, Y, J, Z), f32),
            pltpu.VMEM((X, Y, Z), f32),
            pltpu.VMEM((STEPS, C, 2, Y, J, Z), f32),
            pltpu.VMEM((STEPS, C, 2, X, J, Z), f32),
            pltpu.VMEM((STEPS, C, 2, 8, X * Y * J), f32),
            pltpu.VMEM((STEPS, C, 2, 8, X * Y * J), f32),
            pltpu.VMEM((2, Y, Z), f32),
            pltpu.VMEM((2, X, J, Z), f32),
            pltpu.VMEM((2, 8, X * Y * J), f32),
            pltpu.VMEM((2, 8, X * Y * J), f32),
            pltpu.VMEM((2, 3, 2, X, Y, J, Z), f32),
            pltpu.VMEM((ny, rows, K), f32),
            pltpu.VMEM((ny, rows, K), f32),
            pltpu.VMEM((nx, rows, K), f32),
            pltpu.VMEM((nz, rows, K), f32),
            pltpu.VMEM((3, rows, K), f32),
            pltpu.VMEM((ny, rows, K), f32),
            pltpu.VMEM((nx * ny, STEPS * J, K), f32),
            pltpu.VMEM((nz, STEPS * J, K), f32),
            pltpu.VMEM((nx * ny, 2 * J, K), f32),
            pltpu.VMEM((nz, 2 * J, K), f32),
            pltpu.VMEM((2, STEPS * J, K), f32),
            pltpu.VMEM((2, 2 * J, K), f32),
            pltpu.SemaphoreType.DMA((STEPS * C + 1, 6)),
            pltpu.SemaphoreType.DMA((STEPS * C + 1, 6)),
            pltpu.SemaphoreType.DMA((4, max(sizes))),
            pltpu.SemaphoreType.DMA((4, max(sizes))),
            pltpu.SemaphoreType.DMA((2, 2, most)),
            pltpu.SemaphoreType.DMA((2, 2, most)),
        ],
        compiler_params=pltpu.CompilerParams(
            collective_id=0, has_side_effects=True, vmem_limit_bytes=66650000),
        cost_estimate=pl.CostEstimate(flops=1000000000, bytes_accessed=3000000, transcendentals=0),
    )(basis, now, prev, material_ids, moduli, drive_mask, drive)
    disp, modes, coefs, factors = pl.pallas_call(
        write_out,
        out_shape=shapes,
        in_specs=[hbm] * 4,
        out_specs=(hbm,) * 4,
        scratch_shapes=[pltpu.VMEM(shape.shape, f32) for shape in shapes] + [
            pltpu.SemaphoreType.DMA((4,)), pltpu.SemaphoreType.DMA((4,))],
        compiler_params=pltpu.CompilerParams(vmem_limit_bytes=66650000),
    )(*results)
    return disp, modes, jnp.swapaxes(coefs, 2, 3), factors


def solution(mesh):
    sizes = tuple(mesh.shape[axis] for axis in AXES)
    in_specs = (
        P("gx", None, "gy", "gz", None),
        P(),
        P(),
        P("gx", "gy", "gz"),
        P(),
        P(None, "gx", "gy", "gz"),
        P(),
    )
    out_specs = (P(None, None, "gx", "gy", "gz"), P(None, None, "gx", "gy", "gz"), P(), P())
    return jax.shard_map(functools.partial(shards, sizes), mesh=mesh, in_specs=in_specs,
                         out_specs=out_specs, check_vma=False)
```
